128 devices in a mesh: section: 4 (over z), seq: 32 (over x, y, core).
Axes of the slice: x: 4, y: 4, z: 4, core: 2. Of those that a mesh axis runs over, the one named last changes fastest.
Arguments:
- projected: bfloat16 [4, 3, 16384, 3072], P('section', None, 'seq'), may hold values from -24 to 24
- gate: bfloat16 [4, 3072], P('section'), may hold values from 2 to 8
- head_class: int32 [24], replicated, may hold values 0 or 1
- tile_lists: int32 [2, 128, 8], replicated, may hold values from 0 to 127, as said below
- tile_counts: int32 [24, 128], replicated, may hold values from 1 to 8, as said below
Outputs:
- next_input: bfloat16 [4, 16384, 3072], P('section', 'seq')
The draws below stay inside these ranges and needn't reach their ends.
Inputs may be any that keep to these rules, and one draw needn't show every extreme that they name: tile_lists[c, t, 0] = t, and the 8 entries of a row are distinct tiles. `tile_counts`: counts differ strongly from head to head.
All inputs are finite; a program needn't handle non-finite values.
Results may differ from the reference program's by a relative error of at most 0.0057.
Values may be sent and summed in bfloat16 or wider, within the bound.
No kernel may reach another device: no remote copies, remote signals or barrier semaphores. Data moves between devices by JAX's collectives and lax.ppermute only.
A program may use at most 128 MiB of HBM per device.

```python
import jax
import jax.numpy as jnp
from jax import lax

H = 24
HD = 128
D = 3072
KMAX = 8
QG = 8
MICRO = 4
TOKENS = 16384
NT = 128
FT = 16
WIN = 15


def draw_projected(key, part):
    key = jax.random.fold_in(key, 11)
    base_key = jax.random.fold_in(key, 0)
    factors = jnp.array([1.7, 1.7, 1.0], jnp.float32)[None, :, None, None]
    fields = jax.random.normal(base_key, (MICRO, 3, TOKENS, D), jnp.float32) * factors
    return jnp.clip(fields, -24.0, 24.0).astype(jnp.bfloat16)


def draw_tile_lists(key, part):
    key = jax.random.fold_in(key, 23)
    near_key, far_key = jax.random.split(key)
    positions = jnp.arange(NT, dtype=jnp.int32)[:, None]
    near = jax.vmap(lambda subkey: jax.random.permutation(subkey, WIN))(jax.random.split(near_key, NT))
    near = near[:, :KMAX - 1].astype(jnp.int32) + 1
    far = jax.vmap(lambda subkey: jax.random.permutation(subkey, KMAX - 1))(jax.random.split(far_key, NT))
    far = (far.astype(jnp.int32) + 1) * FT
    zero_col = jnp.zeros((NT, 1), jnp.int32)
    spatial = (positions + jnp.concatenate([zero_col, near], axis=1)) % NT
    temporal = (positions + jnp.concatenate([zero_col, far], axis=1)) % NT
    return jnp.stack([spatial, temporal]).astype(jnp.int32)


def draw_tile_counts(key, part):
    key = jax.random.fold_in(key, 37)
    order_key, count_key = jax.random.split(key)
    order = jax.random.permutation(order_key, H).astype(jnp.int32)
    caps = 1 + order * (KMAX - 1) // (H - 1)
    drawn = jax.random.randint(count_key, (H, NT), 1, caps[:, None] + 1)
    return jnp.where(jnp.arange(NT)[None, :] == 0, caps[:, None], drawn).astype(jnp.int32)


def place_ends(entries, rng, low, high):
    longest = entries.shape.index(max(entries.shape))
    spots = []
    for shift in (0, 1):
        where = [jax.random.randint(jax.random.fold_in(rng, axis), (), 0, length) for axis, length in enumerate(entries.shape)]
        where[longest] = (where[longest] + shift) % entries.shape[longest]
        spots.append(tuple(where))
    return entries.at[spots[0]].set(low).at[spots[1]].set(high)


def levels(own_key, extent, cuts, low, largest):
    factor_of = 1.0
    for position, blocks in cuts:
        draws = jax.random.uniform(jax.random.fold_in(jax.random.fold_in(own_key, 6), position), (blocks,), jnp.float32, low / len(cuts), largest / len(cuts))
        factor_of = factor_of * jnp.repeat(jnp.exp(draws), extent[position] // blocks).reshape((-1,) + (1,) * (len(extent) - 1 - position))
    return factor_of


def setup_inputs(seed: int = 0) -> dict:
    keys = jax.random.split(jax.random.key(seed), 6)
    projected = draw_projected(jax.random.fold_in(keys[5], 71), 0)
    gate = jnp.clip(2.0 + 6.0 * jax.random.uniform(keys[1], (MICRO, D), jnp.float32) ** levels(keys[1], (MICRO, D), ((0, 4),), -0.2, 0.2), 2.0, 8.0).astype(jnp.bfloat16)
    head_class = place_ends((jax.random.randint(keys[2], (H,), 0, 2) < 1).astype(jnp.int32), jax.random.fold_in(keys[2], 1), 0, 1)
    tile_lists = draw_tile_lists(jax.random.fold_in(keys[5], 71), 0)
    tile_counts = draw_tile_counts(jax.random.fold_in(keys[5], 71), 0)
    return {"projected": projected, "gate": gate, "head_class": head_class, "tile_lists": tile_lists, "tile_counts": tile_counts}


def attend_tiles(queries, key_rows, value_rows, tile_rows, counts):
    ntiles = tile_rows.shape[0]
    kmax = tile_rows.shape[1]
    depth = queries.shape[1]
    tile_len = queries.shape[0] // ntiles
    scale_factor = depth ** -0.5
    query_tiles = queries.reshape(ntiles, tile_len, depth)
    key_tiles = key_rows.reshape(ntiles, tile_len, depth)
    value_tiles = value_rows.reshape(ntiles, tile_len, depth)

    def one_group(group):
        offset = (group * QG).astype(jnp.int32)
        group_queries = lax.dynamic_slice_in_dim(query_tiles, offset, QG, 0)
        group_rows = lax.dynamic_slice_in_dim(tile_rows, offset, QG, 0)
        group_counts = lax.dynamic_slice_in_dim(counts, offset, QG, 0)
        gathered_keys = key_tiles[group_rows].reshape(QG, kmax * tile_len, depth)
        gathered_values = value_tiles[group_rows].reshape(QG, kmax * tile_len, depth)
        scores = jnp.einsum("qtd,qkd->qtk", group_queries.astype(jnp.float32), gathered_keys.astype(jnp.float32)) * scale_factor
        usable = jnp.arange(kmax, dtype=jnp.int32)[None, :] < group_counts[:, None]
        usable = jnp.repeat(usable, tile_len, axis=1)[:, None, :]
        scores = jnp.where(usable, scores, -jnp.inf)
        highest = jnp.max(scores, axis=-1, keepdims=True)
        raised = jnp.exp(scores - highest)
        weights = (raised / jnp.sum(raised, axis=-1, keepdims=True)).astype(jnp.bfloat16)
        mixed = jnp.einsum("qtk,qkd->qtd", weights.astype(jnp.float32), gathered_values.astype(jnp.float32))
        return mixed.astype(jnp.bfloat16)

    grouped = lax.map(one_group, jnp.arange(ntiles // QG, dtype=jnp.int32))
    return grouped.reshape(ntiles * tile_len, depth)


def reference(projected, gate, head_class, tile_lists, tile_counts):
    batches = projected.shape[0]
    per_head = projected.reshape(batches, 3, TOKENS, H, HD).transpose(0, 3, 1, 2, 4).reshape(batches * H, 3, TOKENS, HD)
    head_lists = jnp.tile(tile_lists[head_class], (batches, 1, 1))
    head_counts = jnp.tile(tile_counts, (batches, 1))

    def attend_member(member):
        fields, tile_rows, counts = member
        return attend_tiles(fields[0], fields[1], fields[2], tile_rows, counts)

    results = lax.map(attend_member, (per_head, head_lists, head_counts))
    attended = results.reshape(batches, H, TOKENS, HD).transpose(0, 2, 1, 3).reshape(batches, TOKENS, H * HD)
    gated = (gate.astype(jnp.float32)[:, None, :] * attended.astype(jnp.float32)).astype(jnp.bfloat16)
    return jnp.roll(gated, 1, axis=0)
```

```python
import jax
import jax.numpy as jnp
from jax import lax
from jax.experimental import pallas as pl
from jax.experimental.pallas import tpu as pltpu
from jax.sharding import PartitionSpec as P

H = 24
HD = 128
TILE = 128
KMAX = 8
SHARED = 8
PAIRS = 8
CHIPS = 16
SLOTS = 2 * CHIPS
LOG2E = 1.4426950408889634


def pack_kernel(counts_ref, x_ref, out_ref, slot_ref, used_ref, sems):
    loads = jnp.sum(counts_ref[...].astype(jnp.float32), axis=1, keepdims=True)
    order = lax.broadcasted_iota(jnp.int32, (H, 1), 0).astype(jnp.float32)
    keys = loads * 32.0 + (31.0 - order)

    def clear(h, carry):
        used_ref[h] = 0
        return carry

    lax.fori_loop(0, H, clear, 0)
    for k in range(SHARED):
        top = jnp.max(keys)
        keys = jnp.where(keys == top, -1.0, keys)
        head = 31 - lax.rem(top.astype(jnp.int32), 32)
        used_ref[head] = 1
        slot_ref[2 * k + 1] = head
        slot_ref[2 * (k + SHARED) + 1] = head

    def place(h, filled):
        slot_ref[2 * filled] = h
        return filled + 1 - used_ref[h]

    lax.fori_loop(0, H, place, 0)
    copies = []
    for s in range(SLOTS):
        column = pl.multiple_of(slot_ref[s] * HD, HD)
        copy = pltpu.make_async_copy(x_ref.at[:, :, pl.ds(column, HD)], out_ref.at[s], sems.at[s])
        copy.start()
        copies.append(copy)
    for copy in copies:
        copy.wait()


def pack(counts, x):
    return pl.pallas_call(
        pack_kernel,
        out_shape=(
            jax.ShapeDtypeStruct((SLOTS, 3, x.shape[1], HD), x.dtype),
            jax.ShapeDtypeStruct((SLOTS + 8,), jnp.int32),
        ),
        in_specs=[pl.BlockSpec(memory_space=pltpu.VMEM), pl.BlockSpec(memory_space=pl.ANY)],
        out_specs=(pl.BlockSpec(memory_space=pl.ANY), pl.BlockSpec(memory_space=pltpu.SMEM)),
        scratch_shapes=[pltpu.SMEM((H,), jnp.int32), pltpu.SemaphoreType.DMA((SLOTS,))],
        cost_estimate=pl.CostEstimate(flops=0, bytes_accessed=25_000_000, transcendentals=0),
        name="pack_heads",
    )(counts, x)


def attend_kernel(
    slot_ref, class_ref, lists_ref, counts_ref, gate_ref, x_ref,
    first_ref, second_ref, rest_ref,
    held, result, sorted_ref, start_ref, in_sems, out_sems,
):
    pieces = in_sems.shape[0]
    width = x_ref.shape[0] // pieces
    loads = [
        pltpu.make_async_copy(
            x_ref.at[pl.ds(i * width, width)], held.at[pl.ds(i * width, width)], in_sems.at[i]
        )
        for i in range(pieces)
    ]
    for load in loads:
        load.start()

    me = lax.axis_index("seq")
    shared = lax.rem(me, 2)
    parity = me // (2 * SHARED)
    head = slot_ref[me]
    list_base = class_ref[head] * (TILE * KMAX)
    count_base = head * TILE
    ntiles = x_ref.shape[0] * 4

    for c in range(KMAX + 2):
        start_ref[c] = 0
    step = 1 + shared
    total = ntiles // step

    def tally(i, carry):
        count = counts_ref[count_base + i * step + shared * parity]
        start_ref[count + 1] = start_ref[count + 1] + 1
        return carry

    lax.fori_loop(0, total, tally, 0)
    begins = [jnp.int32(0)]
    for c in range(1, KMAX + 1):
        begins.append(begins[-1] + start_ref[c + 1])
    for c in range(1, KMAX + 1):
        start_ref[c] = begins[c - 1]

    def place(i, carry):
        tile = i * step + shared * parity
        count = counts_ref[count_base + tile]
        position = start_ref[count]
        sorted_ref[position] = tile
        start_ref[count] = position + 1
        return carry

    lax.fori_loop(0, total, place, 0)
    gate = gate_ref[:, pl.ds(pl.multiple_of(head * HD, HD), HD)].astype(jnp.float32)
    ones = jnp.ones((TILE, HD), jnp.bfloat16)
    for load in loads:
        load.wait()

    def tile_of(which, t):
        return held[t // 4, which, lax.rem(t, 4)]

    for c in range(1, KMAX + 1):
        group = max(1, PAIRS // c)
        begin, end = begins[c - 1], begins[c]

        def unit(i, carry, c=c, group=group, begin=begin, end=end):
            tiles = [
                sorted_ref[jnp.minimum(begin + i * group + u, end - 1)] for u in range(group)
            ]
            listed = [[lists_ref[list_base + t * KMAX + j] for j in range(c)] for t in tiles]
            scores = [
                lax.dot_general(
                    tile_of(0, t),
                    jnp.concatenate([tile_of(1, k) for k in keys], axis=0),
                    (((1,), (1,)), ((), ())),
                    preferred_element_type=jnp.float32,
                )
                for t, keys in zip(tiles, listed)
            ]
            raised = [
                jnp.exp2((s - jnp.max(s, axis=1, keepdims=True)) * (HD ** (-0.5) * LOG2E)).astype(
                    jnp.bfloat16
                )
                for s in scores
            ]
            mixed = [
                jnp.dot(
                    r,
                    jnp.concatenate(
                        [jnp.concatenate([tile_of(2, k), ones], axis=1) for k in keys], axis=0
                    ),
                    preferred_element_type=jnp.float32,
                )
                for r, keys in zip(raised, listed)
            ]
            for t, m in zip(tiles, mixed):
                attended = (m[:, :HD] / m[:, HD:]).astype(jnp.bfloat16)
                row = lax.rem(t, 4) - shared * parity
                result[row, t // 4] = (gate * attended.astype(jnp.float32)).astype(jnp.bfloat16)
            return carry

        lax.fori_loop(0, (end - begin + group - 1) // group, unit, 0)

    stores = [
        pltpu.make_async_copy(result.at[0], first_ref, out_sems.at[0]),
        pltpu.make_async_copy(result.at[1], second_ref, out_sems.at[1]),
        pltpu.make_async_copy(result.at[2], rest_ref.at[:, 0], out_sems.at[2]),
        pltpu.make_async_copy(result.at[3], rest_ref.at[:, 1], out_sems.at[3]),
    ]
    for store in stores:
        store.start()
    for store in stores:
        store.wait()


def attend(slots, head_class, lists, counts, gate, arrived):
    owners = arrived.shape[0]
    smem = pl.BlockSpec(memory_space=pltpu.SMEM)
    anywhere = pl.BlockSpec(memory_space=pl.ANY)
    part = jax.ShapeDtypeStruct((owners, TILE, HD), jnp.bfloat16)
    return pl.pallas_call(
        attend_kernel,
        out_shape=(part, part, jax.ShapeDtypeStruct((owners, 2, TILE, HD), jnp.bfloat16)),
        in_specs=[smem, smem, smem, smem, pl.BlockSpec(memory_space=pltpu.VMEM), anywhere],
        out_specs=(anywhere, anywhere, anywhere),
        scratch_shapes=[
            pltpu.VMEM(arrived.shape, jnp.bfloat16),
            pltpu.VMEM((4, owners, TILE, HD), jnp.bfloat16),
            pltpu.SMEM((owners * 4,), jnp.int32),
            pltpu.SMEM((KMAX + 2,), jnp.int32),
            pltpu.SemaphoreType.DMA((8,)),
            pltpu.SemaphoreType.DMA((4,)),
        ],
        compiler_params=pltpu.CompilerParams(vmem_limit_bytes=32 * 1024 * 1024),
        cost_estimate=pl.CostEstimate(
            flops=20_000_000_000, bytes_accessed=17_000_000, transcendentals=8_000_000
        ),
        name="attend_tiles",
    )(slots, head_class, lists, counts, gate, arrived)


def row_copies(slot_ref, rows_ref, out_ref, sems):
    copies = []
    for chip in range(CHIPS):
        column = pl.multiple_of(slot_ref[2 * chip] * HD, HD)
        for i in range(2):
            copies.append((rows_ref.at[2 * chip, i], i, column))
        column = pl.multiple_of(slot_ref[2 * chip + 1] * HD, HD)
        copies.append((rows_ref.at[2 * chip + 1, 0], chip // SHARED, column))
    return [
        pltpu.make_async_copy(
            source, out_ref.at[pl.ds(i * TILE, TILE), pl.ds(column, HD)], sems.at[n]
        )
        for n, (source, i, column) in enumerate(copies)
    ]


def unpack_kernel(slot_ref, rows_ref, out_ref, sems):
    copies = row_copies(slot_ref, rows_ref, out_ref, sems)
    for copy in copies:
        copy.start()
    for copy in copies:
        copy.wait()


def unpack(slots, rows):
    anywhere = pl.BlockSpec(memory_space=pl.ANY)
    return pl.pallas_call(
        unpack_kernel,
        out_shape=jax.ShapeDtypeStruct((2 * TILE, H * HD), rows.dtype),
        in_specs=[pl.BlockSpec(memory_space=pltpu.SMEM), anywhere],
        out_specs=anywhere,
        scratch_shapes=[pltpu.SemaphoreType.DMA((3 * CHIPS,))],
        cost_estimate=pl.CostEstimate(flops=0, bytes_accessed=3_000_000, transcendentals=0),
        name="unpack_rows",
    )(slots, rows)


def join_kernel(slot_ref, rows_ref, done_ref, out_ref, sems):
    half = 2 * TILE
    copies = row_copies(slot_ref, rows_ref, out_ref, sems)
    copies.append(
        pltpu.make_async_copy(done_ref, out_ref.at[pl.ds(half, half)], sems.at[len(copies)])
    )
    for copy in copies:
        copy.start()
    for copy in copies:
        copy.wait()


def join(slots, rows, done):
    anywhere = pl.BlockSpec(memory_space=pl.ANY)
    return pl.pallas_call(
        join_kernel,
        out_shape=jax.ShapeDtypeStruct((4 * TILE, H * HD), rows.dtype),
        in_specs=[pl.BlockSpec(memory_space=pltpu.SMEM), anywhere, anywhere],
        out_specs=anywhere,
        scratch_shapes=[pltpu.SemaphoreType.DMA((3 * CHIPS + 1,))],
        cost_estimate=pl.CostEstimate(flops=0, bytes_accessed=6_000_000, transcendentals=0),
        name="join_rows",
    )(slots, rows, done)


def next_section(block, senders):
    sections = lax.axis_size("section")
    owners = lax.axis_size("seq")
    route = [
        (z * owners + s, (z + 1) % sections * owners + s)
        for z in range(sections)
        for s in senders
    ]
    return lax.ppermute(block, ("section", "seq"), route)


def local(projected, gate, head_class, tile_lists, tile_counts):
    owners = lax.axis_size("seq")
    packed, slots = pack(tile_counts, projected[0])
    arrived = lax.all_to_all(packed, "seq", split_axis=0, concat_axis=0, tiled=True)
    arrived = arrived.reshape(owners, 3, 4, TILE, HD)
    first, second, rest = attend(
        slots, head_class, tile_lists.reshape(-1), tile_counts.reshape(-1), gate, arrived
    )
    first = next_section(first, range(owners))
    second = next_section(second, range(0, owners, 2))
    rest = lax.all_to_all(rest, "seq", split_axis=0, concat_axis=0, tiled=True)
    rest = next_section(unpack(slots, rest), range(owners))
    moved = lax.all_to_all(
        jnp.stack([first, second], axis=1), "seq", split_axis=0, concat_axis=0, tiled=True
    )
    return join(slots, moved, rest)[None]


def solution(mesh):
    placed = (P("section", None, "seq", None), P("section", None), P(), P(), P())
    return jax.shard_map(
        local, mesh=mesh, in_specs=placed, out_specs=P("section", "seq", None), check_vma=False
    )
```

```python
import jax
import jax.numpy as jnp
from jax import lax
from jax.experimental import pallas as pl
from jax.experimental.pallas import tpu as pltpu
from jax.sharding import PartitionSpec as P

H = 24
HD = 128
TILE = 128
KMAX = 8
SHARED = 8
PAIRS = 8
CHIPS = 16
SLOTS = 2 * CHIPS
LOG2E = 1.4426950408889634


def pack_kernel(counts_ref, x_ref, out_ref, slot_ref, held, used_ref, in_sems, sems):
    rows = x_ref.shape[1] // 2
    arrivals = []
    for n in range(6):
        part = (n // 2, pl.ds(n % 2 * rows, rows))
        arrivals.append(pltpu.make_async_copy(x_ref.at[part], held.at[part], in_sems.at[n]))
        arrivals[-1].start()
    loads = jnp.sum(counts_ref[...].astype(jnp.float32), axis=1, keepdims=True)
    order = lax.broadcasted_iota(jnp.int32, (H, 1), 0).astype(jnp.float32)
    keys = loads * 32.0 + (31.0 - order)

    def clear(h, carry):
        used_ref[h] = 0
        return carry

    lax.fori_loop(0, H, clear, 0)
    for k in range(SHARED):
        top = jnp.max(keys)
        keys = jnp.where(keys == top, -1.0, keys)
        head = 31 - lax.rem(top.astype(jnp.int32), 32)
        used_ref[head] = 1
        slot_ref[2 * k + 1] = head
        slot_ref[2 * (k + SHARED) + 1] = head

    def place(h, filled):
        slot_ref[2 * filled] = h
        return filled + 1 - used_ref[h]

    lax.fori_loop(0, H, place, 0)
    for arrival in arrivals:
        arrival.wait()
    copies = []
    for s in range(SLOTS):
        column = pl.multiple_of(slot_ref[s] * HD, HD)
        copy = pltpu.make_async_copy(held.at[:, :, pl.ds(column, HD)], out_ref.at[s], sems.at[s])
        copy.start()
        copies.append(copy)
    for copy in copies:
        copy.wait()


def pack(counts, x):
    return pl.pallas_call(
        pack_kernel,
        out_shape=(
            jax.ShapeDtypeStruct((SLOTS, 3, x.shape[1], HD), x.dtype),
            jax.ShapeDtypeStruct((SLOTS + 8,), jnp.int32),
        ),
        in_specs=[pl.BlockSpec(memory_space=pltpu.VMEM), pl.BlockSpec(memory_space=pl.ANY)],
        out_specs=(pl.BlockSpec(memory_space=pl.ANY), pl.BlockSpec(memory_space=pltpu.SMEM)),
        scratch_shapes=[
            pltpu.VMEM(x.shape, x.dtype),
            pltpu.SMEM((H,), jnp.int32),
            pltpu.SemaphoreType.DMA((6,)),
            pltpu.SemaphoreType.DMA((SLOTS,)),
        ],
        compiler_params=pltpu.CompilerParams(vmem_limit_bytes=32 * 1024 * 1024),
        cost_estimate=pl.CostEstimate(flops=0, bytes_accessed=25_000_000, transcendentals=0),
        name="pack_heads",
    )(counts, x)


def attend_kernel(
    slot_ref, class_ref, lists_ref, counts_ref, gate_ref, x_ref,
    first_ref, second_ref, rest_ref,
    held, result, sorted_ref, start_ref, in_sems, out_sems,
):
    pieces = in_sems.shape[0]
    width = x_ref.shape[0] // pieces
    loads = [
        pltpu.make_async_copy(
            x_ref.at[pl.ds(i * width, width)], held.at[pl.ds(i * width, width)], in_sems.at[i]
        )
        for i in range(pieces)
    ]
    for load in loads:
        load.start()

    me = lax.axis_index("seq")
    shared = lax.rem(me, 2)
    parity = me // (2 * SHARED)
    head = slot_ref[me]
    list_base = class_ref[head] * KMAX
    ntiles = x_ref.shape[0] * 4

    for c in range(KMAX + 2):
        start_ref[c] = 0
    step = 1 + shared
    total = ntiles // step

    def tally(i, carry):
        count = counts_ref[head, i * step + shared * parity]
        start_ref[count + 1] = start_ref[count + 1] + 1
        return carry

    lax.fori_loop(0, total, tally, 0)
    begins = [jnp.int32(0)]
    for c in range(1, KMAX + 1):
        begins.append(begins[-1] + start_ref[c + 1])
    for c in range(1, KMAX + 1):
        start_ref[c] = begins[c - 1]

    def place(i, carry):
        tile = i * step + shared * parity
        count = counts_ref[head, tile]
        position = start_ref[count]
        sorted_ref[position] = tile
        start_ref[count] = position + 1
        return carry

    lax.fori_loop(0, total, place, 0)
    gate = gate_ref[:, pl.ds(pl.multiple_of(head * HD, HD), HD)].astype(jnp.float32)
    ones = jnp.ones((TILE, HD), jnp.bfloat16)
    for load in loads:
        load.wait()

    def tile_of(which, t):
        return held[t // 4, which, lax.rem(t, 4)]

    for c in range(1, KMAX + 1):
        group = max(1, PAIRS // c)
        begin, end = begins[c - 1], begins[c]

        def unit(i, carry, c=c, group=group, begin=begin, end=end):
            tiles = [
                sorted_ref[jnp.minimum(begin + i * group + u, end - 1)] for u in range(group)
            ]
            listed = [[lists_ref[list_base + j, t] for j in range(c)] for t in tiles]
            scores = [
                lax.dot_general(
                    tile_of(0, t),
                    jnp.concatenate([tile_of(1, k) for k in keys], axis=0),
                    (((1,), (1,)), ((), ())),
                    preferred_element_type=jnp.float32,
                )
                for t, keys in zip(tiles, listed)
            ]
            raised = [
                jnp.exp2((s - jnp.max(s, axis=1, keepdims=True)) * (HD ** (-0.5) * LOG2E)).astype(
                    jnp.bfloat16
                )
                for s in scores
            ]
            mixed = [
                jnp.dot(
                    r,
                    jnp.concatenate(
                        [jnp.concatenate([tile_of(2, k), ones], axis=1) for k in keys], axis=0
                    ),
                    preferred_element_type=jnp.float32,
                )
                for r, keys in zip(raised, listed)
            ]
            for t, m in zip(tiles, mixed):
                attended = (m[:, :HD] / m[:, HD:]).astype(jnp.bfloat16)
                row = lax.rem(t, 4) - shared * parity
                result[row, t // 4] = (gate * attended.astype(jnp.float32)).astype(jnp.bfloat16)
            return carry

        lax.fori_loop(0, (end - begin + group - 1) // group, unit, 0)

    stores = [
        pltpu.make_async_copy(result.at[0], first_ref, out_sems.at[0]),
        pltpu.make_async_copy(result.at[1], second_ref, out_sems.at[1]),
        pltpu.make_async_copy(result.at[2], rest_ref.at[:, 0], out_sems.at[2]),
        pltpu.make_async_copy(result.at[3], rest_ref.at[:, 1], out_sems.at[3]),
    ]
    for store in stores:
        store.start()
    for store in stores:
        store.wait()


def attend(slots, head_class, lists, counts, gate, arrived):
    owners = arrived.shape[0]
    smem = pl.BlockSpec(memory_space=pltpu.SMEM)
    anywhere = pl.BlockSpec(memory_space=pl.ANY)
    part = jax.ShapeDtypeStruct((owners, TILE, HD), jnp.bfloat16)
    return pl.pallas_call(
        attend_kernel,
        out_shape=(part, part, jax.ShapeDtypeStruct((owners, 2, TILE, HD), jnp.bfloat16)),
        in_specs=[smem, smem, smem, smem, pl.BlockSpec(memory_space=pltpu.VMEM), anywhere],
        out_specs=(anywhere, anywhere, anywhere),
        scratch_shapes=[
            pltpu.VMEM(arrived.shape, jnp.bfloat16),
            pltpu.VMEM((4, owners, TILE, HD), jnp.bfloat16),
            pltpu.SMEM((owners * 4,), jnp.int32),
            pltpu.SMEM((KMAX + 2,), jnp.int32),
            pltpu.SemaphoreType.DMA((8,)),
            pltpu.SemaphoreType.DMA((4,)),
        ],
        compiler_params=pltpu.CompilerParams(vmem_limit_bytes=32 * 1024 * 1024),
        cost_estimate=pl.CostEstimate(
            flops=20_000_000_000, bytes_accessed=17_000_000, transcendentals=8_000_000
        ),
        name="attend_tiles",
    )(slots, head_class, lists, counts, gate, arrived)


def place_rows(slot_ref, rows_ref, out_ref):
    def one_chip(chip, carry):
        columns = pl.ds(pl.multiple_of(slot_ref[2 * chip] * HD, HD), HD)
        for i in range(2):
            out_ref[i * TILE : (i + 1) * TILE, columns] = rows_ref[2 * chip, i]
        columns = pl.ds(pl.multiple_of(slot_ref[2 * chip + 1] * HD, HD), HD)
        start = pl.multiple_of(chip // SHARED * TILE, TILE)
        out_ref[pl.ds(start, TILE), columns] = rows_ref[2 * chip + 1, 0]
        return carry

    lax.fori_loop(0, CHIPS, one_chip, 0)


def join_kernel(slot_ref, rows_ref, done_ref, out_ref):
    place_rows(slot_ref, rows_ref, out_ref)
    half = done_ref.shape[0]
    out_ref[half:, :] = done_ref[...]


def stack_kernel(first_ref, second_ref, after_ref, out_ref):
    out_ref[:, 0] = first_ref[...]
    out_ref[:, 1] = second_ref[...]


def copy_kernel(in_ref, out_ref):
    out_ref[...] = in_ref[...]


def on_vmem(body, shape, kinds, name, moved):
    return pl.pallas_call(
        body,
        out_shape=jax.ShapeDtypeStruct(shape, jnp.bfloat16),
        in_specs=[pl.BlockSpec(memory_space=kind) for kind in kinds],
        out_specs=pl.BlockSpec(memory_space=pltpu.VMEM),
        compiler_params=pltpu.CompilerParams(vmem_limit_bytes=32 * 1024 * 1024),
        cost_estimate=pl.CostEstimate(flops=0, bytes_accessed=moved, transcendentals=0),
        name=name,
    )


def next_section(block, senders):
    sections = lax.axis_size("section")
    owners = lax.axis_size("seq")
    route = [
        (z * owners + s, (z + 1) % sections * owners + s)
        for z in range(sections)
        for s in senders
    ]
    return lax.ppermute(block, ("section", "seq"), route)


def local(projected, gate, head_class, tile_lists, tile_counts):
    owners = lax.axis_size("seq")
    packed, slots = pack(tile_counts, projected[0])
    arrived = lax.all_to_all(packed, "seq", split_axis=0, concat_axis=0, tiled=True)
    arrived = arrived.reshape(owners, 3, 4, TILE, HD)
    lists = tile_lists.transpose(0, 2, 1).reshape(-1, tile_lists.shape[1])
    first, second, rest = attend(slots, head_class, lists, tile_counts, gate, arrived)
    first = next_section(first, range(owners))
    second = next_section(second, range(0, owners, 2))
    smem, vmem = pltpu.SMEM, pltpu.VMEM
    rest = on_vmem(copy_kernel, rest.shape, [vmem], "ready_rows", 4_000_000)(rest)
    rest = lax.all_to_all(rest, "seq", split_axis=0, concat_axis=0, tiled=True)
    half = (2 * TILE, H * HD)
    done = on_vmem(place_rows, half, [smem, vmem], "place_rows", 4_000_000)(slots, rest)
    done = next_section(done, range(owners))
    stacked = on_vmem(stack_kernel, rest.shape, [vmem, vmem, pl.ANY], "stack_rows", 4_000_000)(
        first, second, rest
    )
    moved = lax.all_to_all(stacked, "seq", split_axis=0, concat_axis=0, tiled=True)
    whole = (2 * half[0], half[1])
    return on_vmem(join_kernel, whole, [smem, vmem, vmem], "join_rows", 6_000_000)(
        slots, moved, done
    )[None]


def solution(mesh):
    placed = (P("section", None, "seq", None), P("section", None), P(), P(), P())
    return jax.shard_map(
        local, mesh=mesh, in_specs=placed, out_specs=P("section", "seq", None), check_vma=False
    )
```

```python
import jax
import jax.numpy as jnp
from jax import lax
from jax.experimental import pallas as pl
from jax.experimental.pallas import tpu as pltpu
from jax.sharding import PartitionSpec as P

H = 24
HD = 128
TILE = 128
KMAX = 8
SHARED = 8
PAIRS = 32
CHIPS = 16
SLOTS = 2 * CHIPS
LOG2E = 1.4426950408889634


def pack_kernel(counts_ref, x_ref, out_ref, slot_ref, held, used_ref, in_sems, sems):
    rows = x_ref.shape[1] // 2
    arrivals = []
    for n in range(6):
        part = (n // 2, pl.ds(n % 2 * rows, rows))
        arrivals.append(pltpu.make_async_copy(x_ref.at[part], held.at[part], in_sems.at[n]))
        arrivals[-1].start()
    loads = jnp.sum(counts_ref[...].astype(jnp.float32), axis=1, keepdims=True)
    order = lax.broadcasted_iota(jnp.int32, (H, 1), 0).astype(jnp.float32)
    keys = loads * 32.0 + (31.0 - order)

    def clear(h, carry):
        used_ref[h] = 0
        return carry

    lax.fori_loop(0, H, clear, 0)
    for k in range(SHARED):
        top = jnp.max(keys)
        keys = jnp.where(keys == top, -1.0, keys)
        head = 31 - lax.rem(top.astype(jnp.int32), 32)
        used_ref[head] = 1
        slot_ref[2 * k + 1] = head
        slot_ref[2 * (k + SHARED) + 1] = head

    def place(h, filled):
        slot_ref[2 * filled] = h
        return filled + 1 - used_ref[h]

    lax.fori_loop(0, H, place, 0)
    copies = []
    for which in range(3):
        arrivals[2 * which].wait()
        arrivals[2 * which + 1].wait()
        for s in range(SLOTS):
            columns = pl.ds(pl.multiple_of(slot_ref[s] * HD, HD), HD)
            copy = pltpu.make_async_copy(
                held.at[which, :, columns], out_ref.at[s, which], sems.at[which, s]
            )
            copy.start()
            copies.append(copy)
    for copy in copies:
        copy.wait()


def pack(counts, x):
    return pl.pallas_call(
        pack_kernel,
        out_shape=(
            jax.ShapeDtypeStruct((SLOTS, 3, x.shape[1], HD), x.dtype),
            jax.ShapeDtypeStruct((SLOTS + 8,), jnp.int32),
        ),
        in_specs=[pl.BlockSpec(memory_space=pltpu.VMEM), pl.BlockSpec(memory_space=pl.ANY)],
        out_specs=(pl.BlockSpec(memory_space=pl.ANY), pl.BlockSpec(memory_space=pltpu.SMEM)),
        scratch_shapes=[
            pltpu.VMEM(x.shape, x.dtype),
            pltpu.SMEM((H,), jnp.int32),
            pltpu.SemaphoreType.DMA((6,)),
            pltpu.SemaphoreType.DMA((3, SLOTS)),
        ],
        compiler_params=pltpu.CompilerParams(vmem_limit_bytes=60 * 1024 * 1024),
        cost_estimate=pl.CostEstimate(flops=0, bytes_accessed=25_000_000, transcendentals=0),
        name="pack_heads",
    )(counts, x)


def attend_kernel(
    slot_ref, class_ref, lists_ref, counts_ref, gate_ref, x_ref,
    first_ref, second_ref, rest_ref,
    held, result, sorted_ref, start_ref, in_sems, out_sems,
):
    pieces = in_sems.shape[0]
    width = x_ref.shape[0] // pieces
    loads = [
        pltpu.make_async_copy(
            x_ref.at[pl.ds(i * width, width)], held.at[pl.ds(i * width, width)], in_sems.at[i]
        )
        for i in range(pieces)
    ]
    for load in loads:
        load.start()

    me = lax.axis_index("seq")
    shared = lax.rem(me, 2)
    parity = me // (2 * SHARED)
    head = slot_ref[me]
    list_base = class_ref[head] * KMAX
    ntiles = x_ref.shape[0] * 4

    for c in range(KMAX + 2):
        start_ref[c] = 0
    step = 1 + shared
    total = ntiles // step

    def tally(i, carry):
        count = counts_ref[head, i * step + shared * parity]
        start_ref[count + 1] = start_ref[count + 1] + 1
        return carry

    lax.fori_loop(0, total // 8, lambda i, carry: [tally(8 * i + u, 0) for u in range(8)][-1], 0)
    begins = [jnp.int32(0)]
    for c in range(1, KMAX + 1):
        begins.append(begins[-1] + start_ref[c + 1])
    for c in range(1, KMAX + 1):
        start_ref[c] = begins[c - 1]

    def place(i, carry):
        tile = i * step + shared * parity
        count = counts_ref[head, tile]
        position = start_ref[count]
        sorted_ref[position] = tile
        start_ref[count] = position + 1
        return carry

    lax.fori_loop(0, total // 8, lambda i, carry: [place(8 * i + u, 0) for u in range(8)][-1], 0)
    gate = gate_ref[:, pl.ds(pl.multiple_of(head * HD, HD), HD)].astype(jnp.float32)
    ones = jnp.ones((TILE, HD), jnp.bfloat16)
    for load in loads:
        load.wait()

    def tile_of(which, t):
        return held[t // 4, which, lax.rem(t, 4)]

    for c in range(1, KMAX + 1):
        group = max(1, PAIRS // c)
        begin, end = begins[c - 1], begins[c]

        def unit(i, carry, c=c, group=group, begin=begin, end=end):
            tiles = [
                sorted_ref[jnp.minimum(begin + i * group + u, end - 1)] for u in range(group)
            ]
            listed = [[lists_ref[list_base + j, t] for j in range(c)] for t in tiles]
            scores = [
                lax.dot_general(
                    tile_of(0, t),
                    jnp.concatenate([tile_of(1, k) for k in keys], axis=0),
                    (((1,), (1,)), ((), ())),
                    preferred_element_type=jnp.float32,
                )
                for t, keys in zip(tiles, listed)
            ]
            raised = [
                jnp.exp2((s - jnp.max(s, axis=1, keepdims=True)) * (HD ** (-0.5) * LOG2E)).astype(
                    jnp.bfloat16
                )
                for s in scores
            ]
            mixed = [
                jnp.dot(
                    r,
                    jnp.concatenate(
                        [jnp.concatenate([tile_of(2, k), ones], axis=1) for k in keys], axis=0
                    ),
                    preferred_element_type=jnp.float32,
                )
                for r, keys in zip(raised, listed)
            ]
            for t, m in zip(tiles, mixed):
                attended = (m[:, :HD] / m[:, HD:]).astype(jnp.bfloat16)
                row = lax.rem(t, 4) - shared * parity
                result[row, t // 4] = (gate * attended.astype(jnp.float32)).astype(jnp.bfloat16)
            return carry

        lax.fori_loop(0, (end - begin + group - 1) // group, unit, 0)

    stores = [
        pltpu.make_async_copy(result.at[0], first_ref, out_sems.at[0]),
        pltpu.make_async_copy(result.at[1], second_ref, out_sems.at[1]),
        pltpu.make_async_copy(result.at[2], rest_ref.at[:, 0], out_sems.at[2]),
        pltpu.make_async_copy(result.at[3], rest_ref.at[:, 1], out_sems.at[3]),
    ]
    for store in stores:
        store.start()
    for store in stores:
        store.wait()


def attend(slots, head_class, lists, counts, gate, arrived):
    owners = arrived.shape[0]
    smem = pl.BlockSpec(memory_space=pltpu.SMEM)
    anywhere = pl.BlockSpec(memory_space=pl.ANY)
    part = jax.ShapeDtypeStruct((owners, TILE, HD), jnp.bfloat16)
    return pl.pallas_call(
        attend_kernel,
        out_shape=(part, part, jax.ShapeDtypeStruct((owners, 2, TILE, HD), jnp.bfloat16)),
        in_specs=[smem, smem, smem, smem, pl.BlockSpec(memory_space=pltpu.VMEM), anywhere],
        out_specs=(anywhere, anywhere, anywhere),
        scratch_shapes=[
            pltpu.VMEM(arrived.shape, jnp.bfloat16),
            pltpu.VMEM((4, owners, TILE, HD), jnp.bfloat16),
            pltpu.SMEM((owners * 4,), jnp.int32),
            pltpu.SMEM((KMAX + 2,), jnp.int32),
            pltpu.SemaphoreType.DMA((8,)),
            pltpu.SemaphoreType.DMA((4,)),
        ],
        compiler_params=pltpu.CompilerParams(vmem_limit_bytes=32 * 1024 * 1024),
        cost_estimate=pl.CostEstimate(
            flops=20_000_000_000, bytes_accessed=17_000_000, transcendentals=8_000_000
        ),
        name="attend_tiles",
    )(slots, head_class, lists, counts, gate, arrived)


def place_rows(slot_ref, rows_ref, out_ref):
    def one_chip(chip, carry):
        columns = pl.ds(pl.multiple_of(slot_ref[2 * chip] * HD, HD), HD)
        for i in range(2):
            out_ref[i * TILE : (i + 1) * TILE, columns] = rows_ref[2 * chip, i]
        columns = pl.ds(pl.multiple_of(slot_ref[2 * chip + 1] * HD, HD), HD)
        start = pl.multiple_of(chip // SHARED * TILE, TILE)
        out_ref[pl.ds(start, TILE), columns] = rows_ref[2 * chip + 1, 0]
        return carry

    lax.fori_loop(0, CHIPS, one_chip, 0)


def join_kernel(slot_ref, rows_ref, done_ref, out_ref):
    place_rows(slot_ref, rows_ref, out_ref)
    half = done_ref.shape[0]
    out_ref[half:, :] = done_ref[...]


def stack_kernel(first_ref, second_ref, after_ref, out_ref):
    out_ref[:, 0] = first_ref[...]
    out_ref[:, 1] = second_ref[...]


def on_vmem(body, shape, kinds, name, moved):
    return pl.pallas_call(
        body,
        out_shape=jax.ShapeDtypeStruct(shape, jnp.bfloat16),
        in_specs=[pl.BlockSpec(memory_space=kind) for kind in kinds],
        out_specs=pl.BlockSpec(memory_space=pltpu.VMEM),
        compiler_params=pltpu.CompilerParams(vmem_limit_bytes=32 * 1024 * 1024),
        cost_estimate=pl.CostEstimate(flops=0, bytes_accessed=moved, transcendentals=0),
        name=name,
    )


def next_section(block, senders):
    sections = lax.axis_size("section")
    owners = lax.axis_size("seq")
    route = [
        (z * owners + s, (z + 1) % sections * owners + s)
        for z in range(sections)
        for s in senders
    ]
    return lax.ppermute(block, ("section", "seq"), route)


def local(projected, gate, head_class, tile_lists, tile_counts):
    owners = lax.axis_size("seq")
    packed, slots = pack(tile_counts, projected[0])
    arrived = lax.all_to_all(packed, "seq", split_axis=0, concat_axis=0, tiled=True)
    arrived = arrived.reshape(owners, 3, 4, TILE, HD)
    lists = tile_lists.transpose(0, 2, 1).reshape(-1, tile_lists.shape[1])
    first, second, rest = attend(slots, head_class, lists, tile_counts, gate, arrived)
    first = next_section(first, range(owners))
    second = next_section(second, range(0, owners, 2))
    smem, vmem = pltpu.SMEM, pltpu.VMEM
    rest = lax.all_to_all(rest, "seq", split_axis=0, concat_axis=0, tiled=True)
    half = (2 * TILE, H * HD)
    done = on_vmem(place_rows, half, [smem, vmem], "place_rows", 4_000_000)(slots, rest)
    stacked = on_vmem(stack_kernel, rest.shape, [vmem, vmem, pl.ANY], "stack_rows", 4_000_000)(
        first, second, done
    )
    done = next_section(done, range(owners))
    moved = lax.all_to_all(stacked, "seq", split_axis=0, concat_axis=0, tiled=True)
    whole = (2 * half[0], half[1])
    return on_vmem(join_kernel, whole, [smem, vmem, vmem], "join_rows", 6_000_000)(
        slots, moved, done
    )[None]


def solution(mesh):
    placed = (P("section", None, "seq", None), P("section", None), P(), P(), P())
    return jax.shard_map(
        local, mesh=mesh, in_specs=placed, out_specs=P("section", "seq", None), check_vma=False
    )
```

```python
import jax
import jax.numpy as jnp
from jax import lax
from jax.experimental import pallas as pl
from jax.experimental.pallas import tpu as pltpu
from jax.sharding import PartitionSpec as P

H = 24
HD = 128
TILE = 128
KMAX = 8
SHARED = 8
PAIRS = 32
CHIPS = 16
SLOTS = 2 * CHIPS
SPARE = 1
LONG = 2_000_000_000
LOG2E = 1.4426950408889634


def pack_kernel(counts_ref, x_ref, out_ref, slot_ref, held, used_ref, in_sems, sems):
    rows = x_ref.shape[1] // 2
    arrivals = []
    for n in range(6):
        part = (n // 2, pl.ds(n % 2 * rows, rows))
        arrivals.append(pltpu.make_async_copy(x_ref.at[part], held.at[part], in_sems.at[n]))
        arrivals[-1].start()
    loads = jnp.sum(counts_ref[...].astype(jnp.float32), axis=1, keepdims=True)
    order = lax.broadcasted_iota(jnp.int32, (H, 1), 0).astype(jnp.float32)
    keys = loads * 32.0 + (31.0 - order)

    def clear(h, carry):
        used_ref[h] = 0
        return carry

    lax.fori_loop(0, H, clear, 0)
    for k in range(SHARED):
        top = jnp.max(keys)
        keys = jnp.where(keys == top, -1.0, keys)
        head = 31 - lax.rem(top.astype(jnp.int32), 32)
        used_ref[head] = 1
        slot_ref[2 * k + 1] = head
        slot_ref[2 * (k + SHARED) + 1] = head

    def place(h, filled):
        slot_ref[2 * filled] = h
        return filled + 1 - used_ref[h]

    lax.fori_loop(0, H, place, 0)
    copies = []
    for which in range(3):
        arrivals[2 * which].wait()
        arrivals[2 * which + 1].wait()
        for s in range(SLOTS):
            columns = pl.ds(pl.multiple_of(slot_ref[s] * HD, HD), HD)
            copy = pltpu.make_async_copy(
                held.at[which, :, columns], out_ref.at[s, which], sems.at[which, s]
            )
            copy.start()
            copies.append(copy)
    for copy in copies:
        copy.wait()


def pack(counts, x):
    return pl.pallas_call(
        pack_kernel,
        out_shape=(
            jax.ShapeDtypeStruct((SLOTS, 3, x.shape[1], HD), x.dtype),
            jax.ShapeDtypeStruct((SLOTS + 8,), jnp.int32),
        ),
        in_specs=[pl.BlockSpec(memory_space=pltpu.VMEM), pl.BlockSpec(memory_space=pl.ANY)],
        out_specs=(pl.BlockSpec(memory_space=pl.ANY), pl.BlockSpec(memory_space=pltpu.SMEM)),
        scratch_shapes=[
            pltpu.VMEM(x.shape, x.dtype),
            pltpu.SMEM((H,), jnp.int32),
            pltpu.SemaphoreType.DMA((6,)),
            pltpu.SemaphoreType.DMA((3, SLOTS)),
        ],
        compiler_params=pltpu.CompilerParams(vmem_limit_bytes=60 * 1024 * 1024),
        cost_estimate=pl.CostEstimate(flops=0, bytes_accessed=25_000_000, transcendentals=0),
        name="pack_heads",
    )(counts, x)


def attend_kernel(
    slot_ref, class_ref, lists_ref, counts_ref, gate_ref, x_ref,
    pair_ref, single_ref, rest_ref,
    held, result, sorted_ref, start_ref, in_sems, out_sems,
):
    pieces = in_sems.shape[0]
    owners = x_ref.shape[0]
    width = x_ref.shape[0] // pieces
    loads = [
        pltpu.make_async_copy(
            x_ref.at[pl.ds(i * width, width)], held.at[pl.ds(i * width, width)], in_sems.at[i]
        )
        for i in range(pieces)
    ]
    for load in loads:
        load.start()

    me = lax.axis_index("seq")
    shared = lax.rem(me, 2)
    parity = me // (2 * SHARED)
    head = slot_ref[me]
    list_base = class_ref[head] * KMAX
    ntiles = x_ref.shape[0] * 4

    for c in range(KMAX + 2):
        start_ref[c] = 0
    step = 1 + shared
    total = ntiles // step

    def tally(i, carry):
        count = counts_ref[head, i * step + shared * parity]
        start_ref[count + 1] = start_ref[count + 1] + 1
        return carry

    lax.fori_loop(0, total // 8, lambda i, carry: [tally(8 * i + u, 0) for u in range(8)][-1], 0)
    begins = [jnp.int32(0)]
    for c in range(1, KMAX + 1):
        begins.append(begins[-1] + start_ref[c + 1])
    for c in range(1, KMAX + 1):
        start_ref[c] = begins[c - 1]

    def place(i, carry):
        tile = i * step + shared * parity
        count = counts_ref[head, tile]
        position = start_ref[count]
        sorted_ref[position] = tile
        start_ref[count] = position + 1
        return carry

    lax.fori_loop(0, total // 8, lambda i, carry: [place(8 * i + u, 0) for u in range(8)][-1], 0)
    gate = gate_ref[:, pl.ds(pl.multiple_of(head * HD, HD), HD)].astype(jnp.float32)
    ones = jnp.ones((TILE, HD), jnp.bfloat16)
    for load in loads:
        load.wait()

    def tile_of(which, t):
        return held[t // 4, which, lax.rem(t, 4)]

    for c in range(1, KMAX + 1):
        group = max(1, PAIRS // c)
        begin, end = begins[c - 1], begins[c]

        def unit(i, carry, c=c, group=group, begin=begin, end=end):
            tiles = [
                sorted_ref[jnp.minimum(begin + i * group + u, end - 1)] for u in range(group)
            ]
            listed = [[lists_ref[list_base + j, t] for j in range(c)] for t in tiles]
            scores = [
                lax.dot_general(
                    tile_of(0, t),
                    jnp.concatenate([tile_of(1, k) for k in keys], axis=0),
                    (((1,), (1,)), ((), ())),
                    preferred_element_type=jnp.float32,
                )
                for t, keys in zip(tiles, listed)
            ]
            raised = [
                jnp.exp2((s - jnp.max(s, axis=1, keepdims=True)) * (HD ** (-0.5) * LOG2E)).astype(
                    jnp.bfloat16
                )
                for s in scores
            ]
            mixed = [
                jnp.dot(
                    r,
                    jnp.concatenate(
                        [jnp.concatenate([tile_of(2, k), ones], axis=1) for k in keys], axis=0
                    ),
                    preferred_element_type=jnp.float32,
                )
                for r, keys in zip(raised, listed)
            ]
            for t, m in zip(tiles, mixed):
                attended = (m[:, :HD] / m[:, HD:]).astype(jnp.bfloat16)
                row = lax.rem(t, 4) - shared * parity
                result[row, t // 4] = (gate * attended.astype(jnp.float32)).astype(jnp.bfloat16)
            return carry

        lax.fori_loop(0, (end - begin + group - 1) // group, unit, 0)

    stores = [
        pltpu.make_async_copy(result.at[0], pair_ref.at[pl.ds(0, owners), 0], out_sems.at[0]),
        pltpu.make_async_copy(result.at[1], pair_ref.at[pl.ds(0, owners), 1], out_sems.at[1]),
        pltpu.make_async_copy(result.at[2], rest_ref.at[:, 0], out_sems.at[2]),
        pltpu.make_async_copy(result.at[3], rest_ref.at[:, 1], out_sems.at[3]),
        pltpu.make_async_copy(result.at[0], single_ref, out_sems.at[4]),
    ]
    for store in stores:
        store.start()
    for store in stores:
        store.wait()


def attend(slots, head_class, lists, counts, gate, arrived):
    owners = arrived.shape[0]
    smem = pl.BlockSpec(memory_space=pltpu.SMEM)
    anywhere = pl.BlockSpec(memory_space=pl.ANY)
    part = jax.ShapeDtypeStruct((owners, TILE, HD), jnp.bfloat16)
    pair = jax.ShapeDtypeStruct((owners + SPARE, 2, TILE, HD), jnp.bfloat16)
    return pl.pallas_call(
        attend_kernel,
        out_shape=(pair, part, jax.ShapeDtypeStruct((owners, 2, TILE, HD), jnp.bfloat16)),
        in_specs=[smem, smem, smem, smem, pl.BlockSpec(memory_space=pltpu.VMEM), anywhere],
        out_specs=(anywhere, anywhere, anywhere),
        scratch_shapes=[
            pltpu.VMEM(arrived.shape, jnp.bfloat16),
            pltpu.VMEM((4, owners, TILE, HD), jnp.bfloat16),
            pltpu.SMEM((owners * 4,), jnp.int32),
            pltpu.SMEM((KMAX + 2,), jnp.int32),
            pltpu.SemaphoreType.DMA((8,)),
            pltpu.SemaphoreType.DMA((5,)),
        ],
        compiler_params=pltpu.CompilerParams(vmem_limit_bytes=60 * 1024 * 1024),
        cost_estimate=pl.CostEstimate(
            flops=20_000_000_000, bytes_accessed=17_000_000, transcendentals=8_000_000
        ),
        name="attend_tiles",
    )(slots, head_class, lists, counts, gate, arrived)


def place_rows(slot_ref, rows_ref, out_ref):
    def one_chip(chip, carry):
        columns = pl.ds(pl.multiple_of(slot_ref[2 * chip] * HD, HD), HD)
        for i in range(2):
            out_ref[i * TILE : (i + 1) * TILE, columns] = rows_ref[2 * chip, i]
        columns = pl.ds(pl.multiple_of(slot_ref[2 * chip + 1] * HD, HD), HD)
        start = pl.multiple_of(chip // SHARED * TILE, TILE)
        out_ref[pl.ds(start, TILE), columns] = rows_ref[2 * chip + 1, 0]
        return carry

    lax.fori_loop(0, CHIPS, one_chip, 0)


def stack_kernel(pair_ref, single_ref, out_ref):
    shared = lax.rem(lax.axis_index("seq"), 2)
    owners = single_ref.shape[0]

    @pl.when(shared == 0)
    def _():
        out_ref[...] = pair_ref[:owners]

    @pl.when(shared == 1)
    def _():
        out_ref[:, 0] = single_ref[...]


def after_kernel(in_ref, before_ref, out_ref):
    pass


def lay_kernel(done_ref, out_ref, sem):
    half = done_ref.shape[0]
    copy = pltpu.make_async_copy(done_ref, out_ref.at[pl.ds(half, half)], sem)
    copy.start()
    copy.wait()


def join_kernel(slot_ref, rows_ref, laid_ref, out_ref, half_ref, sem):
    place_rows(slot_ref, rows_ref, half_ref)
    copy = pltpu.make_async_copy(half_ref, out_ref.at[pl.ds(0, half_ref.shape[0])], sem)
    copy.start()
    copy.wait()


def small_call(body, shape, kinds, name, cost=4_000_000, kind=pltpu.VMEM, **more):
    return pl.pallas_call(
        body,
        out_shape=jax.ShapeDtypeStruct(shape, jnp.bfloat16),
        in_specs=[pl.BlockSpec(memory_space=k) for k in kinds],
        out_specs=pl.BlockSpec(memory_space=kind),
        compiler_params=pltpu.CompilerParams(vmem_limit_bytes=60 * 1024 * 1024),
        cost_estimate=pl.CostEstimate(flops=cost * 10000 if cost > 1e8 else 0, bytes_accessed=cost, transcendentals=0),
        name=name,
        **more,
    )


def next_section(block, senders):
    sections = lax.axis_size("section")
    owners = lax.axis_size("seq")
    route = [
        (z * owners + s, (z + 1) % sections * owners + s)
        for z in range(sections)
        for s in senders
    ]
    return lax.ppermute(block, ("section", "seq"), route)


def local(projected, gate, head_class, tile_lists, tile_counts):
    owners = lax.axis_size("seq")
    packed, slots = pack(tile_counts, projected[0])
    arrived = lax.all_to_all(packed, "seq", split_axis=0, concat_axis=0, tiled=True)
    arrived = arrived.reshape(owners, 3, 4, TILE, HD)
    lists = tile_lists.transpose(0, 2, 1).reshape(-1, tile_lists.shape[1])
    pair, single, rest = attend(slots, head_class, lists, tile_counts, gate, arrived)
    pair = next_section(pair, range(0, owners, 2))
    single = next_section(single, range(1, owners, 2))
    smem, vmem = pltpu.SMEM, pltpu.VMEM
    stacked = small_call(stack_kernel, rest.shape, [vmem, vmem], "stack_rows", LONG)(pair, single)
    rest = lax.all_to_all(rest, "seq", split_axis=0, concat_axis=0, tiled=True)
    half = (2 * TILE, H * HD)
    done = small_call(place_rows, half, [smem, vmem], "place_rows",1000)(slots, rest)
    stacked = small_call(
        after_kernel, rest.shape, [pl.ANY, pl.ANY], "rows_after", 1000, pl.ANY,
        input_output_aliases={0: 0},
    )(stacked, done)
    done = next_section(done, range(owners))
    whole = (2 * half[0], half[1])
    dma = pltpu.SemaphoreType.DMA
    laid = small_call(
        lay_kernel, whole, [vmem], "lay_rows", LONG, pl.ANY, scratch_shapes=[dma]
    )(done)
    moved = lax.all_to_all(stacked, "seq", split_axis=0, concat_axis=0, tiled=True)
    return small_call(
        join_kernel, whole, [smem, vmem, pl.ANY], "join_rows", kind=pl.ANY,
        input_output_aliases={2: 0}, scratch_shapes=[vmem(half, jnp.bfloat16), dma],
    )(slots, moved, laid)[None]


def solution(mesh):
    placed = (P("section", None, "seq", None), P("section", None), P(), P(), P())
    return jax.shard_map(
        local, mesh=mesh, in_specs=placed, out_specs=P("section", "seq", None), check_vma=False
    )
```

```python
import jax
import jax.numpy as jnp
from jax import lax
from jax.experimental import pallas as pl
from jax.experimental.pallas import tpu as pltpu
from jax.sharding import PartitionSpec as P

H = 24
HD = 128
TILE = 128
KMAX = 8
SHARED = 8
PAIRS = 32
CHIPS = 16
SLOTS = 2 * CHIPS
LONG = 20_000_000_000_000
LOG2E = 1.4426950408889634


def pack_kernel(counts_ref, x_ref, out_ref, slot_ref, held, used_ref, in_sems, sems):
    rows = x_ref.shape[1] // 2
    arrivals = []
    for n in range(6):
        part = (n // 2, pl.ds(n % 2 * rows, rows))
        arrivals.append(pltpu.make_async_copy(x_ref.at[part], held.at[part], in_sems.at[n]))
        arrivals[-1].start()
    loads = jnp.sum(counts_ref[...].astype(jnp.float32), axis=1, keepdims=True)
    order = lax.broadcasted_iota(jnp.int32, (H, 1), 0).astype(jnp.float32)
    keys = loads * 32.0 + (31.0 - order)

    def clear(h, carry):
        used_ref[h] = 0
        return carry

    lax.fori_loop(0, H, clear, 0)
    for k in range(SHARED):
        top = jnp.max(keys)
        keys = jnp.where(keys == top, -1.0, keys)
        head = 31 - lax.rem(top.astype(jnp.int32), 32)
        used_ref[head] = 1
        slot_ref[2 * k + 1] = head
        slot_ref[2 * (k + SHARED) + 1] = head

    def place(h, filled):
        slot_ref[2 * filled] = h
        return filled + 1 - used_ref[h]

    lax.fori_loop(0, H, place, 0)
    copies = []
    for which in range(3):
        arrivals[2 * which].wait()
        arrivals[2 * which + 1].wait()
        for s in range(SLOTS):
            columns = pl.ds(pl.multiple_of(slot_ref[s] * HD, HD), HD)
            copy = pltpu.make_async_copy(
                held.at[which, :, columns], out_ref.at[s, which], sems.at[which, s]
            )
            copy.start()
            copies.append(copy)
    for copy in copies:
        copy.wait()


def pack(counts, x):
    return pl.pallas_call(
        pack_kernel,
        out_shape=(
            jax.ShapeDtypeStruct((SLOTS, 3, x.shape[1], HD), x.dtype),
            jax.ShapeDtypeStruct((SLOTS + 8,), jnp.int32),
        ),
        in_specs=[pl.BlockSpec(memory_space=pltpu.VMEM), pl.BlockSpec(memory_space=pl.ANY)],
        out_specs=(pl.BlockSpec(memory_space=pl.ANY), pl.BlockSpec(memory_space=pltpu.SMEM)),
        scratch_shapes=[
            pltpu.VMEM(x.shape, x.dtype),
            pltpu.SMEM((H,), jnp.int32),
            pltpu.SemaphoreType.DMA((6,)),
            pltpu.SemaphoreType.DMA((3, SLOTS)),
        ],
        compiler_params=pltpu.CompilerParams(vmem_limit_bytes=60 * 1024 * 1024),
        cost_estimate=pl.CostEstimate(flops=0, bytes_accessed=25_000_000, transcendentals=0),
        name="pack_heads",
    )(counts, x)


def attend_kernel(
    slot_ref, class_ref, lists_ref, counts_ref, gate_ref, x_ref,
    pair_ref, single_ref, rest_ref,
    held, result, sorted_ref, start_ref, in_sems, out_sems,
):
    pieces = in_sems.shape[0]
    owners = x_ref.shape[0]
    width = x_ref.shape[0] // pieces
    loads = [
        pltpu.make_async_copy(
            x_ref.at[pl.ds(i * width, width)], held.at[pl.ds(i * width, width)], in_sems.at[i]
        )
        for i in range(pieces)
    ]
    for load in loads:
        load.start()

    me = lax.axis_index("seq")
    shared = lax.rem(me, 2)
    parity = me // (2 * SHARED)
    head = slot_ref[me]
    list_base = class_ref[head] * KMAX
    ntiles = x_ref.shape[0] * 4

    for c in range(KMAX + 2):
        start_ref[c] = 0
    step = 1 + shared
    total = ntiles // step

    def tally(i, carry):
        count = counts_ref[head, i * step + shared * parity]
        start_ref[count + 1] = start_ref[count + 1] + 1
        return carry

    lax.fori_loop(0, total // 8, lambda i, carry: [tally(8 * i + u, 0) for u in range(8)][-1], 0)
    begins = [jnp.int32(0)]
    for c in range(1, KMAX + 1):
        begins.append(begins[-1] + start_ref[c + 1])
    for c in range(1, KMAX + 1):
        start_ref[c] = begins[c - 1]

    def place(i, carry):
        tile = i * step + shared * parity
        count = counts_ref[head, tile]
        position = start_ref[count]
        sorted_ref[position] = tile
        start_ref[count] = position + 1
        return carry

    lax.fori_loop(0, total // 8, lambda i, carry: [place(8 * i + u, 0) for u in range(8)][-1], 0)
    gate = gate_ref[:, pl.ds(pl.multiple_of(head * HD, HD), HD)].astype(jnp.float32)
    ones = jnp.ones((TILE, HD), jnp.bfloat16)
    for load in loads:
        load.wait()

    def tile_of(which, t):
        return held[t // 4, which, lax.rem(t, 4)]

    for c in range(1, KMAX + 1):
        group = max(1, PAIRS // c)
        begin, end = begins[c - 1], begins[c]

        def unit(i, carry, c=c, group=group, begin=begin, end=end):
            tiles = [
                sorted_ref[jnp.minimum(begin + i * group + u, end - 1)] for u in range(group)
            ]
            listed = [[lists_ref[list_base + j, t] for j in range(c)] for t in tiles]
            scores = [
                lax.dot_general(
                    tile_of(0, t),
                    jnp.concatenate([tile_of(1, k) for k in keys], axis=0),
                    (((1,), (1,)), ((), ())),
                    preferred_element_type=jnp.float32,
                )
                for t, keys in zip(tiles, listed)
            ]
            raised = [
                jnp.exp2((s - jnp.max(s, axis=1, keepdims=True)) * (HD ** (-0.5) * LOG2E)).astype(
                    jnp.bfloat16
                )
                for s in scores
            ]
            mixed = [
                jnp.dot(
                    r,
                    jnp.concatenate(
                        [jnp.concatenate([tile_of(2, k), ones], axis=1) for k in keys], axis=0
                    ),
                    preferred_element_type=jnp.float32,
                )
                for r, keys in zip(raised, listed)
            ]
            for t, m in zip(tiles, mixed):
                attended = (m[:, :HD] / m[:, HD:]).astype(jnp.bfloat16)
                row = lax.rem(t, 4) - shared * parity
                result[row, t // 4] = (gate * attended.astype(jnp.float32)).astype(jnp.bfloat16)
            return carry

        lax.fori_loop(0, (end - begin + group - 1) // group, unit, 0)

    sends = [
        (0, pair_ref.at[pl.ds(0, owners), 0], 0),
        (1, pair_ref.at[pl.ds(0, owners), 1], 0),
        (3, rest_ref.at[:, 1], 0),
        (0, single_ref, 1),
        (2, rest_ref.at[:, 0], None),
    ]
    for wait in (False, True):
        for n, (row, target, only) in enumerate(sends):
            store = pltpu.make_async_copy(result.at[row], target, out_sems.at[n])
            act = store.wait if wait else store.start
            if only is None:
                act()
            else:
                pl.when(shared == only)(act)


def attend(slots, head_class, lists, counts, gate, arrived):
    owners = arrived.shape[0]
    smem = pl.BlockSpec(memory_space=pltpu.SMEM)
    anywhere = pl.BlockSpec(memory_space=pl.ANY)
    part = jax.ShapeDtypeStruct((owners, TILE, HD), jnp.bfloat16)
    pair = jax.ShapeDtypeStruct((owners, 2, TILE, HD), jnp.bfloat16)
    return pl.pallas_call(
        attend_kernel,
        out_shape=(pair, part, jax.ShapeDtypeStruct((owners, 2, TILE, HD), jnp.bfloat16)),
        in_specs=[smem, smem, smem, smem, pl.BlockSpec(memory_space=pltpu.VMEM), anywhere],
        out_specs=(anywhere, anywhere, anywhere),
        scratch_shapes=[
            pltpu.VMEM(arrived.shape, jnp.bfloat16),
            pltpu.VMEM((4, owners, TILE, HD), jnp.bfloat16),
            pltpu.SMEM((owners * 4,), jnp.int32),
            pltpu.SMEM((KMAX + 2,), jnp.int32),
            pltpu.SemaphoreType.DMA((8,)),
            pltpu.SemaphoreType.DMA((5,)),
        ],
        compiler_params=pltpu.CompilerParams(vmem_limit_bytes=60 * 1024 * 1024),
        cost_estimate=pl.CostEstimate(
            flops=20_000_000_000, bytes_accessed=17_000_000, transcendentals=8_000_000
        ),
        name="attend_tiles",
    )(slots, head_class, lists, counts, gate, arrived)


def place_rows(slot_ref, rows_ref, out_ref, held, half, in_sems, out_sems):
    pieces = in_sems.shape[0]
    width, chips = rows_ref.shape[0] // pieces, CHIPS // pieces
    loads = [
        pltpu.make_async_copy(
            rows_ref.at[pl.ds(n * width, width)], held.at[pl.ds(n * width, width)], in_sems.at[n]
        )
        for n in range(pieces)
    ]
    for load in loads:
        load.start()
    for n in range(pieces):
        loads[n].wait()

        def one_chip(i, carry, n=n):
            chip = n * chips + i
            columns = pl.ds(pl.multiple_of(slot_ref[2 * chip] * HD, HD), HD)
            half[:TILE, columns] = held[2 * chip, 0]
            half[TILE:, columns] = held[2 * chip, 1]
            columns = pl.ds(pl.multiple_of(slot_ref[2 * chip + 1] * HD, HD), HD)
            start = pl.multiple_of(chip // SHARED * TILE, TILE)
            half[pl.ds(start, TILE), columns] = held[2 * chip + 1, 0]
            return carry

        lax.fori_loop(0, chips, one_chip, 0)
    return send_rows(half, out_ref, out_sems)


def send_rows(source, target, sems):
    pieces = sems.shape[0]
    rows = source.shape[0] // pieces
    copies = [
        pltpu.make_async_copy(
            source.at[pl.ds(n * rows, rows)], target.at[pl.ds(n * rows, rows)], sems.at[n]
        )
        for n in range(pieces)
    ]
    for copy in copies:
        copy.start()
    return copies


def place_kernel(slot_ref, rows_ref, out_ref, held, half, in_sems, out_sems):
    for copy in place_rows(slot_ref, rows_ref, out_ref, held, half, in_sems, out_sems):
        copy.wait()


def join_kernel(
    slot_ref, rows_ref, done_ref, out_ref, held, half, in_sems, out_sems, other, other_sems
):
    arrivals = send_rows(done_ref, other, other_sems.at[0])
    rows = half.shape[0]
    copies = place_rows(slot_ref, rows_ref, out_ref, held, half, in_sems, out_sems)
    for arrival in arrivals:
        arrival.wait()
    copies += send_rows(other, out_ref.at[pl.ds(rows, rows)], other_sems.at[1])
    for copy in copies:
        copy.wait()


def stack_kernel(pair_ref, single_ref, out_ref, held, in_sems, out_sems):
    @pl.when(lax.rem(lax.axis_index("seq"), 2) == 1)
    def _():
        arrivals = send_rows(single_ref, held, in_sems)
        for arrival in arrivals:
            arrival.wait()
        pieces = out_sems.shape[0]
        rows = held.shape[0] // pieces
        copies = [
            pltpu.make_async_copy(
                held.at[pl.ds(n * rows, rows)], out_ref.at[pl.ds(n * rows, rows), 0], out_sems.at[n]
            )
            for n in range(pieces)
        ]
        for copy in copies:
            copy.start()
        for copy in copies:
            copy.wait()


def after_kernel(in_ref, before_ref, out_ref):
    pass


def same_kernel(in_ref, out_ref):
    pass


def small_call(body, shape, kinds, name, kind=pl.ANY, flops=0, **more):
    return pl.pallas_call(
        body,
        out_shape=jax.ShapeDtypeStruct(shape, jnp.bfloat16),
        in_specs=[pl.BlockSpec(memory_space=k) for k in kinds],
        out_specs=pl.BlockSpec(memory_space=kind),
        compiler_params=pltpu.CompilerParams(vmem_limit_bytes=60 * 1024 * 1024),
        cost_estimate=pl.CostEstimate(flops=flops, bytes_accessed=1000, transcendentals=0),
        name=name,
        **more,
    )


def next_section(block, senders):
    sections = lax.axis_size("section")
    owners = lax.axis_size("seq")
    route = [
        (z * owners + s, (z + 1) % sections * owners + s)
        for z in range(sections)
        for s in senders
    ]
    return lax.ppermute(block, ("section", "seq"), route)


def local(projected, gate, head_class, tile_lists, tile_counts):
    owners = lax.axis_size("seq")
    packed, slots = pack(tile_counts, projected[0])
    arrived = lax.all_to_all(packed, "seq", split_axis=0, concat_axis=0, tiled=True)
    arrived = arrived.reshape(owners, 3, 4, TILE, HD)
    lists = tile_lists.transpose(0, 2, 1).reshape(-1, tile_lists.shape[1])
    pair, single, rest = attend(slots, head_class, lists, tile_counts, gate, arrived)
    pair = next_section(pair, range(0, owners, 2))
    single = next_section(single, range(1, owners, 2))
    smem, vmem, dma = pltpu.SMEM, pltpu.VMEM, pltpu.SemaphoreType.DMA
    stacked = small_call(
        stack_kernel, rest.shape, [pl.ANY, pl.ANY], "stack_rows", flops=LONG,
        input_output_aliases={0: 0},
        scratch_shapes=[vmem(single.shape, single.dtype), dma((4,)), dma((4,))],
    )(pair, single)
    rest = lax.all_to_all(rest, "seq", split_axis=0, concat_axis=0, tiled=True)
    half = (2 * TILE, H * HD)
    place_scratch = [vmem(rest.shape, rest.dtype), vmem(half, rest.dtype), dma((4,)), dma((4,))]
    done = small_call(
        place_kernel, half, [smem, pl.ANY], "place_rows", scratch_shapes=place_scratch
    )(slots, rest)
    stacked = small_call(
        after_kernel, rest.shape, [pl.ANY, pl.ANY], "rows_after", input_output_aliases={0: 0}
    )(stacked, done)
    done = next_section(done, range(owners))
    done = small_call(
        same_kernel, half, [pl.ANY], "rows_shifted", flops=LONG, input_output_aliases={0: 0}
    )(done)
    moved = lax.all_to_all(stacked, "seq", split_axis=0, concat_axis=0, tiled=True)
    return small_call(
        join_kernel, (2 * half[0], half[1]), [smem, pl.ANY, pl.ANY], "join_rows",
        scratch_shapes=place_scratch + [vmem(half, rest.dtype), dma((2, 4))],
    )(slots, moved, done)[None]


def solution(mesh):
    placed = (P("section", None, "seq", None), P("section", None), P(), P(), P())
    return jax.shard_map(
        local, mesh=mesh, in_specs=placed, out_specs=P("section", "seq", None), check_vma=False
    )
```

```python
import jax
import jax.numpy as jnp
from jax import lax
from jax.experimental import pallas as pl
from jax.experimental.pallas import tpu as pltpu
from jax.sharding import PartitionSpec as P

H = 24
HD = 128
TILE = 128
KMAX = 8
SHARED = 8
PAIRS = 32
CHIPS = 16
SLOTS = 2 * CHIPS
LONG = 20_000_000_000_000
LOG2E = 1.4426950408889634


def pack_kernel(counts_ref, x_ref, out_ref, slot_ref, held, used_ref, in_sems, sems):
    rows = x_ref.shape[1] // 2
    arrivals = []
    for n in range(6):
        part = (n // 2, pl.ds(n % 2 * rows, rows))
        arrivals.append(pltpu.make_async_copy(x_ref.at[part], held.at[part], in_sems.at[n]))
        arrivals[-1].start()
    loads = jnp.sum(counts_ref[...].astype(jnp.float32), axis=1, keepdims=True)
    order = lax.broadcasted_iota(jnp.int32, (H, 1), 0).astype(jnp.float32)
    keys = loads * 32.0 + (31.0 - order)

    def clear(h, carry):
        used_ref[h] = 0
        return carry

    lax.fori_loop(0, H, clear, 0)
    for k in range(SHARED):
        top = jnp.max(keys)
        keys = jnp.where(keys == top, -1.0, keys)
        head = 31 - lax.rem(top.astype(jnp.int32), 32)
        used_ref[head] = 1
        slot_ref[2 * k + 1] = head
        slot_ref[2 * (k + SHARED) + 1] = head

    def place(h, filled):
        slot_ref[2 * filled] = h
        return filled + 1 - used_ref[h]

    lax.fori_loop(0, H, place, 0)
    copies = []
    for which in range(3):
        arrivals[2 * which].wait()
        arrivals[2 * which + 1].wait()
        for s in range(SLOTS):
            columns = pl.ds(pl.multiple_of(slot_ref[s] * HD, HD), HD)
            copy = pltpu.make_async_copy(
                held.at[which, :, columns], out_ref.at[s, which], sems.at[which, s]
            )
            copy.start()
            copies.append(copy)
    for copy in copies:
        copy.wait()


def pack(counts, x):
    return pl.pallas_call(
        pack_kernel,
        out_shape=(
            jax.ShapeDtypeStruct((SLOTS, 3, x.shape[1], HD), x.dtype),
            jax.ShapeDtypeStruct((SLOTS + 8,), jnp.int32),
        ),
        in_specs=[pl.BlockSpec(memory_space=pltpu.VMEM), pl.BlockSpec(memory_space=pl.ANY)],
        out_specs=(pl.BlockSpec(memory_space=pl.ANY), pl.BlockSpec(memory_space=pltpu.SMEM)),
        scratch_shapes=[
            pltpu.VMEM(x.shape, x.dtype),
            pltpu.SMEM((H,), jnp.int32),
            pltpu.SemaphoreType.DMA((6,)),
            pltpu.SemaphoreType.DMA((3, SLOTS)),
        ],
        compiler_params=pltpu.CompilerParams(vmem_limit_bytes=60 * 1024 * 1024),
        cost_estimate=pl.CostEstimate(flops=0, bytes_accessed=25_000_000, transcendentals=0),
        name="pack_heads",
    )(counts, x)


def attend_kernel(
    slot_ref, class_ref, lists_ref, counts_ref, gate_ref, x_ref,
    pair_ref, single_ref, rest_ref,
    result, sorted_ref, start_ref, out_sems,
):
    owners = x_ref.shape[0]

    me = lax.axis_index("seq")
    shared = lax.rem(me, 2)
    parity = me // (2 * SHARED)
    head = slot_ref[me]
    list_base = class_ref[head] * KMAX
    ntiles = x_ref.shape[0] * 4

    for c in range(KMAX + 2):
        start_ref[c] = 0
    step = 1 + shared
    total = ntiles // step

    def tally(i, carry):
        count = counts_ref[head, i * step + shared * parity]
        start_ref[count + 1] = start_ref[count + 1] + 1
        return carry

    lax.fori_loop(0, total // 8, lambda i, carry: [tally(8 * i + u, 0) for u in range(8)][-1], 0)
    begins = [jnp.int32(0)]
    for c in range(1, KMAX + 1):
        begins.append(begins[-1] + start_ref[c + 1])
    for c in range(1, KMAX + 1):
        start_ref[c] = begins[c - 1]

    def place(i, carry):
        tile = i * step + shared * parity
        count = counts_ref[head, tile]
        position = start_ref[count]
        sorted_ref[position] = tile
        start_ref[count] = position + 1
        return carry

    lax.fori_loop(0, total // 8, lambda i, carry: [place(8 * i + u, 0) for u in range(8)][-1], 0)
    gate = gate_ref[:, pl.ds(pl.multiple_of(head * HD, HD), HD)].astype(jnp.float32)
    ones = jnp.ones((TILE, HD), jnp.bfloat16)

    def tile_of(which, t):
        return x_ref[t // 4, which, lax.rem(t, 4)]

    for c in range(1, KMAX + 1):
        group = max(1, PAIRS // c)
        begin, end = begins[c - 1], begins[c]

        def unit(i, carry, c=c, group=group, begin=begin, end=end):
            tiles = [
                sorted_ref[jnp.minimum(begin + i * group + u, end - 1)] for u in range(group)
            ]
            listed = [[lists_ref[list_base + j, t] for j in range(c)] for t in tiles]
            scores = [
                lax.dot_general(
                    tile_of(0, t),
                    jnp.concatenate([tile_of(1, k) for k in keys], axis=0),
                    (((1,), (1,)), ((), ())),
                    preferred_element_type=jnp.float32,
                )
                for t, keys in zip(tiles, listed)
            ]
            raised = [
                jnp.exp2((s - jnp.max(s, axis=1, keepdims=True)) * (HD ** (-0.5) * LOG2E)).astype(
                    jnp.bfloat16
                )
                for s in scores
            ]
            mixed = [
                jnp.dot(
                    r,
                    jnp.concatenate(
                        [jnp.concatenate([tile_of(2, k), ones], axis=1) for k in keys], axis=0
                    ),
                    preferred_element_type=jnp.float32,
                )
                for r, keys in zip(raised, listed)
            ]
            for t, m in zip(tiles, mixed):
                attended = (m[:, :HD] / m[:, HD:]).astype(jnp.bfloat16)
                row = lax.rem(t, 4) - shared * parity
                result[row, t // 4] = (gate * attended.astype(jnp.float32)).astype(jnp.bfloat16)
            return carry

        lax.fori_loop(0, (end - begin + group - 1) // group, unit, 0)

    sends = [
        (0, pair_ref.at[pl.ds(0, owners), 0], 0),
        (1, pair_ref.at[pl.ds(0, owners), 1], 0),
        (3, rest_ref.at[:, 1], 0),
        (0, single_ref, 1),
        (2, rest_ref.at[:, 0], None),
    ]
    for wait in (False, True):
        for n, (row, target, only) in enumerate(sends):
            store = pltpu.make_async_copy(result.at[row], target, out_sems.at[n])
            act = store.wait if wait else store.start
            if only is None:
                act()
            else:
                pl.when(shared == only)(act)


def attend(slots, head_class, lists, counts, gate, arrived):
    owners = arrived.shape[0]
    smem = pl.BlockSpec(memory_space=pltpu.SMEM)
    vmem = pl.BlockSpec(memory_space=pltpu.VMEM)
    anywhere = pl.BlockSpec(memory_space=pl.ANY)
    part = jax.ShapeDtypeStruct((owners, TILE, HD), jnp.bfloat16)
    pair = jax.ShapeDtypeStruct((owners, 2, TILE, HD), jnp.bfloat16)
    return pl.pallas_call(
        attend_kernel,
        out_shape=(pair, part, jax.ShapeDtypeStruct((owners, 2, TILE, HD), jnp.bfloat16)),
        in_specs=[smem, smem, smem, smem, vmem, vmem],
        out_specs=(anywhere, anywhere, anywhere),
        scratch_shapes=[
            pltpu.VMEM((4, owners, TILE, HD), jnp.bfloat16),
            pltpu.SMEM((owners * 4,), jnp.int32),
            pltpu.SMEM((KMAX + 2,), jnp.int32),
            pltpu.SemaphoreType.DMA((5,)),
        ],
        compiler_params=pltpu.CompilerParams(vmem_limit_bytes=20 * 1024 * 1024),
        cost_estimate=pl.CostEstimate(
            flops=20_000_000_000, bytes_accessed=17_000_000, transcendentals=8_000_000
        ),
        name="attend_tiles",
    )(slots, head_class, lists, counts, gate, arrived)


def place_rows(slot_ref, rows_ref, out_ref, held, half, in_sems, out_sems):
    pieces = in_sems.shape[0]
    width, chips = rows_ref.shape[0] // pieces, CHIPS // pieces
    loads = [
        pltpu.make_async_copy(
            rows_ref.at[pl.ds(n * width, width)], held.at[pl.ds(n * width, width)], in_sems.at[n]
        )
        for n in range(pieces)
    ]
    for load in loads:
        load.start()
    for n in range(pieces):
        loads[n].wait()

        def one_chip(i, carry, n=n):
            chip = n * chips + i
            columns = pl.ds(pl.multiple_of(slot_ref[2 * chip] * HD, HD), HD)
            half[:TILE, columns] = held[2 * chip, 0]
            half[TILE:, columns] = held[2 * chip, 1]
            columns = pl.ds(pl.multiple_of(slot_ref[2 * chip + 1] * HD, HD), HD)
            start = pl.multiple_of(chip // SHARED * TILE, TILE)
            half[pl.ds(start, TILE), columns] = held[2 * chip + 1, 0]
            return carry

        lax.fori_loop(0, chips, one_chip, 0)
    return send_rows(half, out_ref, out_sems)


def send_rows(source, target, sems):
    pieces = sems.shape[0]
    rows = source.shape[0] // pieces
    copies = [
        pltpu.make_async_copy(
            source.at[pl.ds(n * rows, rows)], target.at[pl.ds(n * rows, rows)], sems.at[n]
        )
        for n in range(pieces)
    ]
    for copy in copies:
        copy.start()
    return copies


def place_kernel(slot_ref, rows_ref, out_ref, held, half, in_sems, out_sems):
    for copy in place_rows(slot_ref, rows_ref, out_ref, held, half, in_sems, out_sems):
        copy.wait()


def join_kernel(
    slot_ref, rows_ref, done_ref, out_ref, held, half, in_sems, out_sems, other, other_sems
):
    arrivals = send_rows(done_ref, other, other_sems.at[0])
    rows = half.shape[0]
    copies = place_rows(slot_ref, rows_ref, out_ref, held, half, in_sems, out_sems)
    for arrival in arrivals:
        arrival.wait()
    copies += send_rows(other, out_ref.at[pl.ds(rows, rows)], other_sems.at[1])
    for copy in copies:
        copy.wait()


def stack_kernel(pair_ref, single_ref, out_ref, held, in_sems, out_sems):
    @pl.when(lax.rem(lax.axis_index("seq"), 2) == 1)
    def _():
        arrivals = send_rows(single_ref, held, in_sems)
        for arrival in arrivals:
            arrival.wait()
        pieces = out_sems.shape[0]
        rows = held.shape[0] // pieces
        copies = [
            pltpu.make_async_copy(
                held.at[pl.ds(n * rows, rows)], out_ref.at[pl.ds(n * rows, rows), 0], out_sems.at[n]
            )
            for n in range(pieces)
        ]
        for copy in copies:
            copy.start()
        for copy in copies:
            copy.wait()


def after_kernel(in_ref, before_ref, out_ref):
    pass


def same_kernel(in_ref, out_ref):
    pass


def small_call(body, shape, kinds, name, kind=pl.ANY, flops=0, **more):
    return pl.pallas_call(
        body,
        out_shape=jax.ShapeDtypeStruct(shape, jnp.bfloat16),
        in_specs=[pl.BlockSpec(memory_space=k) for k in kinds],
        out_specs=pl.BlockSpec(memory_space=kind),
        compiler_params=pltpu.CompilerParams(vmem_limit_bytes=60 * 1024 * 1024),
        cost_estimate=pl.CostEstimate(flops=flops, bytes_accessed=1000, transcendentals=0),
        name=name,
        **more,
    )


def next_section(block, senders):
    sections = lax.axis_size("section")
    owners = lax.axis_size("seq")
    route = [
        (z * owners + s, (z + 1) % sections * owners + s)
        for z in range(sections)
        for s in senders
    ]
    return lax.ppermute(block, ("section", "seq"), route)


def local(projected, gate, head_class, tile_lists, tile_counts):
    owners = lax.axis_size("seq")
    packed, slots = pack(tile_counts, projected[0])
    arrived = lax.all_to_all(packed, "seq", split_axis=0, concat_axis=0, tiled=True)
    arrived = arrived.reshape(owners, 3, 4, TILE, HD)
    lists = tile_lists.transpose(0, 2, 1).reshape(-1, tile_lists.shape[1])
    pair, single, rest = attend(slots, head_class, lists, tile_counts, gate, arrived)
    pair = next_section(pair, range(0, owners, 2))
    single = next_section(single, range(1, owners, 2))
    smem, vmem, dma = pltpu.SMEM, pltpu.VMEM, pltpu.SemaphoreType.DMA
    stacked = small_call(
        stack_kernel, rest.shape, [pl.ANY, pl.ANY], "stack_rows", flops=LONG,
        input_output_aliases={0: 0},
        scratch_shapes=[vmem(single.shape, single.dtype), dma((4,)), dma((4,))],
    )(pair, single)
    rest = lax.all_to_all(rest, "seq", split_axis=0, concat_axis=0, tiled=True)
    half = (2 * TILE, H * HD)
    place_scratch = [vmem(rest.shape, rest.dtype), vmem(half, rest.dtype), dma((4,)), dma((4,))]
    done = small_call(
        place_kernel, half, [smem, pl.ANY], "place_rows", scratch_shapes=place_scratch
    )(slots, rest)
    stacked = small_call(
        after_kernel, rest.shape, [pl.ANY, pl.ANY], "rows_after", input_output_aliases={0: 0}
    )(stacked, done)
    done = next_section(done, range(owners))
    done = small_call(
        same_kernel, half, [pl.ANY], "rows_shifted", flops=LONG, input_output_aliases={0: 0}
    )(done)
    moved = lax.all_to_all(stacked, "seq", split_axis=0, concat_axis=0, tiled=True)
    return small_call(
        join_kernel, (2 * half[0], half[1]), [smem, pl.ANY, pl.ANY], "join_rows",
        scratch_shapes=place_scratch + [vmem(half, rest.dtype), dma((2, 4))],
    )(slots, moved, done)[None]


def solution(mesh):
    placed = (P("section", None, "seq", None), P("section", None), P(), P(), P())
    return jax.shard_map(
        local, mesh=mesh, in_specs=placed, out_specs=P("section", "seq", None), check_vma=False
    )
```

```python
import jax
import jax.numpy as jnp
from jax import lax
from jax.experimental import pallas as pl
from jax.experimental.pallas import tpu as pltpu
from jax.sharding import PartitionSpec as P

H = 24
HD = 128
TILE = 128
KMAX = 8
SHARED = 8
PAIRS = 32
CHIPS = 16
SLOTS = 2 * CHIPS
LONG = 20_000_000_000_000
LOG2E = 1.4426950408889634


def pack_kernel(counts_ref, x_ref, out_ref, slot_ref, held, used_ref, in_sems, sems):
    rows = x_ref.shape[1] // 2
    arrivals = []
    for n in range(6):
        part = (n // 2, pl.ds(n % 2 * rows, rows))
        arrivals.append(pltpu.make_async_copy(x_ref.at[part], held.at[part], in_sems.at[n]))
        arrivals[-1].start()
    loads = jnp.sum(counts_ref[...].astype(jnp.float32), axis=1, keepdims=True)
    order = lax.broadcasted_iota(jnp.int32, (H, 1), 0).astype(jnp.float32)
    keys = loads * 32.0 + (31.0 - order)

    def clear(h, carry):
        used_ref[h] = 0
        return carry

    lax.fori_loop(0, H, clear, 0)
    for k in range(SHARED):
        top = jnp.max(keys)
        keys = jnp.where(keys == top, -1.0, keys)
        head = 31 - lax.rem(top.astype(jnp.int32), 32)
        used_ref[head] = 1
        slot_ref[2 * k + 1] = head
        slot_ref[2 * (k + SHARED) + 1] = head

    def place(h, filled):
        slot_ref[2 * filled] = h
        return filled + 1 - used_ref[h]

    lax.fori_loop(0, H, place, 0)
    copies = []
    for which in range(3):
        arrivals[2 * which].wait()
        arrivals[2 * which + 1].wait()
        for s in range(SLOTS):
            columns = pl.ds(pl.multiple_of(slot_ref[s] * HD, HD), HD)
            copy = pltpu.make_async_copy(
                held.at[which, :, columns], out_ref.at[s, which], sems.at[which, s]
            )
            copy.start()
            copies.append(copy)
    for copy in copies:
        copy.wait()


def pack(counts, x):
    return pl.pallas_call(
        pack_kernel,
        out_shape=(
            jax.ShapeDtypeStruct((SLOTS, 3, x.shape[1], HD), x.dtype),
            jax.ShapeDtypeStruct((SLOTS + 8,), jnp.int32),
        ),
        in_specs=[pl.BlockSpec(memory_space=pltpu.VMEM), pl.BlockSpec(memory_space=pl.ANY)],
        out_specs=(pl.BlockSpec(memory_space=pl.ANY), pl.BlockSpec(memory_space=pltpu.SMEM)),
        scratch_shapes=[
            pltpu.VMEM(x.shape, x.dtype),
            pltpu.SMEM((H,), jnp.int32),
            pltpu.SemaphoreType.DMA((6,)),
            pltpu.SemaphoreType.DMA((3, SLOTS)),
        ],
        compiler_params=pltpu.CompilerParams(vmem_limit_bytes=60 * 1024 * 1024),
        cost_estimate=pl.CostEstimate(flops=0, bytes_accessed=25_000_000, transcendentals=0),
        name="pack_heads",
    )(counts, x)


def attend_kernel(
    slot_ref, class_ref, lists_ref, counts_ref, gate_ref, x_ref,
    pair_ref, single_ref, rest_ref,
    result, sorted_ref, start_ref, out_sems,
):
    owners = x_ref.shape[0]

    me = lax.axis_index("seq")
    shared = lax.rem(me, 2)
    parity = me // (2 * SHARED)
    head = slot_ref[me]
    list_base = class_ref[head] * KMAX
    ntiles = x_ref.shape[0] * 4

    for c in range(KMAX + 2):
        start_ref[c] = 0
    step = 1 + shared
    total = ntiles // step

    def tally(i, carry):
        count = counts_ref[head, i * step + shared * parity]
        start_ref[count + 1] = start_ref[count + 1] + 1
        return carry

    lax.fori_loop(0, total // 8, lambda i, carry: [tally(8 * i + u, 0) for u in range(8)][-1], 0)
    begins = [jnp.int32(0)]
    for c in range(1, KMAX + 1):
        begins.append(begins[-1] + start_ref[c + 1])
    for c in range(1, KMAX + 1):
        start_ref[c] = begins[c - 1]

    def place(i, carry):
        tile = i * step + shared * parity
        count = counts_ref[head, tile]
        position = start_ref[count]
        sorted_ref[position] = tile
        start_ref[count] = position + 1
        return carry

    lax.fori_loop(0, total // 8, lambda i, carry: [place(8 * i + u, 0) for u in range(8)][-1], 0)
    gate = gate_ref[:, pl.ds(pl.multiple_of(head * HD, HD), HD)].astype(jnp.float32)
    ones = jnp.ones((TILE, HD), jnp.bfloat16)

    def tile_of(which, t):
        return x_ref[t // 4, which, lax.rem(t, 4)]

    for c in range(1, KMAX + 1):
        group = max(1, PAIRS // c)
        begin, end = begins[c - 1], begins[c]

        def unit(i, carry, c=c, group=group, begin=begin, end=end):
            tiles = [
                sorted_ref[jnp.minimum(begin + i * group + u, end - 1)] for u in range(group)
            ]
            listed = [[lists_ref[list_base + j, t] for j in range(c)] for t in tiles]
            scores = [
                lax.dot_general(
                    tile_of(0, t),
                    jnp.concatenate([tile_of(1, k) for k in keys], axis=0),
                    (((1,), (1,)), ((), ())),
                    preferred_element_type=jnp.float32,
                )
                for t, keys in zip(tiles, listed)
            ]
            raised = [
                jnp.exp2((s - jnp.max(s, axis=1, keepdims=True)) * (HD ** (-0.5) * LOG2E)).astype(
                    jnp.bfloat16
                )
                for s in scores
            ]
            mixed = [
                jnp.dot(
                    r,
                    jnp.concatenate(
                        [jnp.concatenate([tile_of(2, k), ones], axis=1) for k in keys], axis=0
                    ),
                    preferred_element_type=jnp.float32,
                )
                for r, keys in zip(raised, listed)
            ]
            for t, m in zip(tiles, mixed):
                attended = (m[:, :HD] / m[:, HD:]).astype(jnp.bfloat16)
                row = lax.rem(t, 4) - shared * parity
                result[row, t // 4] = (gate * attended.astype(jnp.float32)).astype(jnp.bfloat16)
            return carry

        lax.fori_loop(0, (end - begin + group - 1) // group, unit, 0)

    sends = [
        (0, pair_ref.at[pl.ds(0, owners), 0], 0),
        (1, pair_ref.at[pl.ds(0, owners), 1], 0),
        (3, rest_ref.at[:, 1], 0),
        (0, single_ref, 1),
        (2, rest_ref.at[:, 0], None),
    ]
    for wait in (False, True):
        for n, (row, target, only) in enumerate(sends):
            store = pltpu.make_async_copy(result.at[row], target, out_sems.at[n])
            act = store.wait if wait else store.start
            if only is None:
                act()
            else:
                pl.when(shared == only)(act)


def attend(slots, head_class, lists, counts, gate, arrived):
    owners = arrived.shape[0]
    smem = pl.BlockSpec(memory_space=pltpu.SMEM)
    vmem = pl.BlockSpec(memory_space=pltpu.VMEM)
    anywhere = pl.BlockSpec(memory_space=pl.ANY)
    part = jax.ShapeDtypeStruct((owners, TILE, HD), jnp.bfloat16)
    pair = jax.ShapeDtypeStruct((owners, 2, TILE, HD), jnp.bfloat16)
    return pl.pallas_call(
        attend_kernel,
        out_shape=(pair, part, jax.ShapeDtypeStruct((owners, 2, TILE, HD), jnp.bfloat16)),
        in_specs=[smem, smem, smem, smem, vmem, vmem],
        out_specs=(anywhere, anywhere, anywhere),
        scratch_shapes=[
            pltpu.VMEM((4, owners, TILE, HD), jnp.bfloat16),
            pltpu.SMEM((owners * 4,), jnp.int32),
            pltpu.SMEM((KMAX + 2,), jnp.int32),
            pltpu.SemaphoreType.DMA((5,)),
        ],
        compiler_params=pltpu.CompilerParams(vmem_limit_bytes=20 * 1024 * 1024),
        cost_estimate=pl.CostEstimate(
            flops=20_000_000_000, bytes_accessed=17_000_000, transcendentals=8_000_000
        ),
        name="attend_tiles",
    )(slots, head_class, lists, counts, gate, arrived)


def place_rows(slot_ref, rows_ref, out_ref):
    def one_chip(chip, carry):
        columns = pl.ds(pl.multiple_of(slot_ref[2 * chip] * HD, HD), HD)
        out_ref[:TILE, columns] = rows_ref[2 * chip, 0]
        out_ref[TILE:, columns] = rows_ref[2 * chip, 1]
        columns = pl.ds(pl.multiple_of(slot_ref[2 * chip + 1] * HD, HD), HD)
        start = pl.multiple_of(chip // SHARED * TILE, TILE)
        out_ref[pl.ds(start, TILE), columns] = rows_ref[2 * chip + 1, 0]
        return carry

    lax.fori_loop(0, CHIPS, one_chip, 0)


def send_rows(source, target, sems):
    pieces = sems.shape[0]
    rows = source.shape[0] // pieces
    copies = [
        pltpu.make_async_copy(
            source.at[pl.ds(n * rows, rows)], target.at[pl.ds(n * rows, rows)], sems.at[n]
        )
        for n in range(pieces)
    ]
    for copy in copies:
        copy.start()
    return copies


def join_kernel(slot_ref, rows_ref, done_ref, out_ref, half, sems):
    rows = half.shape[0]
    copies = send_rows(done_ref, out_ref.at[pl.ds(rows, rows)], sems.at[0])
    place_rows(slot_ref, rows_ref, half)
    copies += send_rows(half, out_ref.at[pl.ds(0, rows)], sems.at[1])
    for copy in copies:
        copy.wait()


def stack_kernel(pair_ref, single_ref, out_ref, held, in_sems, out_sems):
    @pl.when(lax.rem(lax.axis_index("seq"), 2) == 1)
    def _():
        arrivals = send_rows(single_ref, held, in_sems)
        for arrival in arrivals:
            arrival.wait()
        pieces = out_sems.shape[0]
        rows = held.shape[0] // pieces
        copies = [
            pltpu.make_async_copy(
                held.at[pl.ds(n * rows, rows)], out_ref.at[pl.ds(n * rows, rows), 0], out_sems.at[n]
            )
            for n in range(pieces)
        ]
        for copy in copies:
            copy.start()
        for copy in copies:
            copy.wait()


def after_kernel(in_ref, before_ref, out_ref):
    pass


def same_kernel(in_ref, out_ref):
    pass


def small_call(body, shape, kinds, name, kind=pl.ANY, flops=0, **more):
    return pl.pallas_call(
        body,
        out_shape=jax.ShapeDtypeStruct(shape, jnp.bfloat16),
        in_specs=[pl.BlockSpec(memory_space=k) for k in kinds],
        out_specs=pl.BlockSpec(memory_space=kind),
        compiler_params=pltpu.CompilerParams(vmem_limit_bytes=16 * 1024 * 1024),
        cost_estimate=pl.CostEstimate(flops=flops, bytes_accessed=1000, transcendentals=0),
        name=name,
        **more,
    )


def next_section(block, senders):
    sections = lax.axis_size("section")
    owners = lax.axis_size("seq")
    route = [
        (z * owners + s, (z + 1) % sections * owners + s)
        for z in range(sections)
        for s in senders
    ]
    return lax.ppermute(block, ("section", "seq"), route)


def local(projected, gate, head_class, tile_lists, tile_counts):
    owners = lax.axis_size("seq")
    packed, slots = pack(tile_counts, projected[0])
    arrived = lax.all_to_all(packed, "seq", split_axis=0, concat_axis=0, tiled=True)
    arrived = arrived.reshape(owners, 3, 4, TILE, HD)
    lists = tile_lists.transpose(0, 2, 1).reshape(-1, tile_lists.shape[1])
    pair, single, rest = attend(slots, head_class, lists, tile_counts, gate, arrived)
    pair = next_section(pair, range(0, owners, 2))
    single = next_section(single, range(1, owners, 2))
    smem, vmem, dma = pltpu.SMEM, pltpu.VMEM, pltpu.SemaphoreType.DMA
    stacked = small_call(
        stack_kernel, rest.shape, [pl.ANY, pl.ANY], "stack_rows", flops=LONG,
        input_output_aliases={0: 0},
        scratch_shapes=[vmem(single.shape, single.dtype), dma((4,)), dma((4,))],
    )(pair, single)
    rest = lax.all_to_all(rest, "seq", split_axis=0, concat_axis=0, tiled=True)
    half = (2 * TILE, H * HD)
    done = small_call(place_rows, half, [smem, vmem], "place_rows", vmem)(slots, rest)
    stacked = small_call(
        after_kernel, rest.shape, [pl.ANY, pl.ANY], "rows_after", input_output_aliases={0: 0}
    )(stacked, done)
    done = next_section(done, range(owners))
    done = small_call(
        same_kernel, half, [pl.ANY], "rows_shifted", flops=LONG, input_output_aliases={0: 0}
    )(done)
    moved = lax.all_to_all(stacked, "seq", split_axis=0, concat_axis=0, tiled=True)
    return small_call(
        join_kernel, (2 * half[0], half[1]), [smem, vmem, vmem], "join_rows",
        scratch_shapes=[vmem(half, rest.dtype), dma((2, 4))],
    )(slots, moved, done)[None]


def solution(mesh):
    placed = (P("section", None, "seq", None), P("section", None), P(), P(), P())
    return jax.shard_map(
        local, mesh=mesh, in_specs=placed, out_specs=P("section", "seq", None), check_vma=False
    )
```
